128 devices in a mesh: seq: 8 (over y_lo, x), res: 16 (over y_hi, z, core).
Axes of the slice: x: 4, y: 4 (y_hi: 2, y_lo: 2; y = y_hi * 2 + y_lo), z: 4, core: 2. Of those that a mesh axis runs over, the one named last changes fastest.
Arguments:
- alignment_input: bfloat16 [128, 512, 768], P('seq', 'res'), may hold values from -6 to 6
- row_query_key_value: bfloat16 [768, 2304], replicated, as said below
- row_output_weight: bfloat16 [768, 768], replicated, may hold values from -0.21875 to 0.21875
- column_query_key_value: bfloat16 [768, 2304], replicated, as said below
- column_output_weight: bfloat16 [768, 768], replicated, may hold values from -0.21875 to 0.21875
- feedforward_input_weight: bfloat16 [768, 3072], replicated, may hold values from -0.21875 to 0.21875
- feedforward_output_weight: bfloat16 [3072, 768], replicated, may hold values from -0.109375 to 0.109375
Outputs:
- layer_out: bfloat16 [128, 512, 768], P('seq', 'res')
The draws below stay inside these ranges and needn't reach their ends.
Inputs may be any that keep to these rules, and one draw needn't show every extreme that they name: `row_query_key_value`: a projection matrix. `column_query_key_value`: a projection matrix.
All inputs are finite; a program needn't handle non-finite values.
Results may differ from the reference program's by a relative error of at most 0.015.
Values may be sent and summed in bfloat16 or wider, within the bound.
No kernel may reach another device: no remote copies, remote signals or barrier semaphores. Data moves between devices by JAX's collectives and lax.ppermute only.
A program may use at most 128 MiB of HBM per device.

```python
import math
import jax
import jax.numpy as jnp
from jax import lax

H = 12
DH = 64
MODEL_DIM = 768
FF = 3072
ALIGNMENT_ROWS = 128
RESIDUE_TOTAL = 512


def drawn_weight(key):
    return jax.random.normal(key, (MODEL_DIM, 3 * MODEL_DIM), jnp.float32) * MODEL_DIM ** (-0.5)


def draw_row_query_key_value(key, part):
    key = jax.random.fold_in(key, 11)
    return drawn_weight(key).astype(jnp.bfloat16)


def draw_column_query_key_value(key, part):
    key = jax.random.fold_in(key, 23)
    return drawn_weight(key).astype(jnp.bfloat16)


def shard_levels(stream_key, dims, shards, least, top_value):
    loudness = 1.0
    for axis_at, parts in shards:
        steps = jax.random.uniform(jax.random.fold_in(jax.random.fold_in(stream_key, 6), axis_at), (parts,), jnp.float32, least / len(shards), top_value / len(shards))
        loudness = loudness * jnp.repeat(jnp.exp(steps), dims[axis_at] // parts).reshape((-1,) + (1,) * (len(dims) - 1 - axis_at))
    return loudness


def noise(rng, dims, spread, limit, cuts=(), dtype=jnp.bfloat16):
    drawn = spread * jax.random.normal(rng, dims, jnp.float32)
    if cuts:
        drawn = drawn * shard_levels(rng, dims, cuts, -0.22, 0.18)
    return jnp.clip(drawn, -limit, limit).astype(dtype)


def setup_inputs(seed: int = 0) -> dict:
    seeds = jax.random.split(jax.random.key(seed), 8)
    return {
        "alignment_input": noise(seeds[0], (ALIGNMENT_ROWS, RESIDUE_TOTAL, MODEL_DIM), 1.0, 6.0, ((0, 8), (1, 16))),
        "row_query_key_value": draw_row_query_key_value(jax.random.fold_in(seeds[7], 71), 0),
        "row_output_weight": noise(seeds[2], (MODEL_DIM, MODEL_DIM), MODEL_DIM ** -0.5, 0.21875),
        "column_query_key_value": draw_column_query_key_value(jax.random.fold_in(seeds[7], 71), 0),
        "column_output_weight": noise(seeds[4], (MODEL_DIM, MODEL_DIM), MODEL_DIM ** -0.5, 0.21875),
        "feedforward_input_weight": noise(seeds[5], (MODEL_DIM, FF), MODEL_DIM ** -0.5, 0.21875),
        "feedforward_output_weight": noise(seeds[6], (FF, MODEL_DIM), FF ** -0.5, 0.109375),
    }


def normalize_rows(values_in):
    wide = values_in.astype(jnp.float32)
    centre = lax.optimization_barrier(jnp.mean(wide, axis=-1, keepdims=True))
    variance = lax.optimization_barrier(jnp.mean((wide - centre) ** 2, axis=-1, keepdims=True))
    return ((wide - centre) * lax.rsqrt(variance + 1e-05)).astype(jnp.bfloat16)

def split_heads(projected):
    rows_n, res_n, triple = projected.shape
    width = triple // 3
    return [projected[:, :, index * width:(index + 1) * width].reshape(rows_n, res_n, H, DH).astype(jnp.float32) for index in range(3)]

def reference(alignment_input, row_query_key_value, row_output_weight, column_query_key_value, column_output_weight, feedforward_input_weight, feedforward_output_weight):
    normalized_first = normalize_rows(alignment_input)
    row_proj = jnp.dot(normalized_first, row_query_key_value, preferred_element_type=jnp.float32).astype(jnp.bfloat16)
    queries, keys, values = split_heads(row_proj)
    row_scores = jnp.einsum('rihc,rjhc->ihj', queries, keys) * (1.0 / math.sqrt(DH * ALIGNMENT_ROWS))
    row_weights = jax.nn.softmax(row_scores, axis=-1).astype(jnp.bfloat16)
    row_attention_output = jnp.einsum('ihj,rjhc->rihc', row_weights.astype(jnp.float32), values).astype(jnp.bfloat16)
    row_attention_output = row_attention_output.reshape(ALIGNMENT_ROWS, RESIDUE_TOTAL, MODEL_DIM)
    state_after_rows = (alignment_input.astype(jnp.float32) + jnp.dot(row_attention_output, row_output_weight, preferred_element_type=jnp.float32)).astype(jnp.bfloat16)
    normed_b = normalize_rows(state_after_rows)
    col_proj = jnp.dot(normed_b, column_query_key_value, preferred_element_type=jnp.float32).astype(jnp.bfloat16)
    queries, keys, values = split_heads(col_proj)
    col_scores = jnp.einsum('rjhc,sjhc->jhrs', queries, keys) * (1.0 / math.sqrt(DH))
    col_weights = jax.nn.softmax(col_scores, axis=-1).astype(jnp.bfloat16)
    col_attended = jnp.einsum('jhrs,sjhc->rjhc', col_weights.astype(jnp.float32), values).astype(jnp.bfloat16)
    col_attended = col_attended.reshape(ALIGNMENT_ROWS, RESIDUE_TOTAL, MODEL_DIM)
    after_cols = (state_after_rows.astype(jnp.float32) + jnp.dot(col_attended, column_output_weight, preferred_element_type=jnp.float32)).astype(jnp.bfloat16)
    hidden = jax.nn.gelu(jnp.dot(normalize_rows(after_cols), feedforward_input_weight, preferred_element_type=jnp.float32)).astype(jnp.bfloat16)
    return (after_cols.astype(jnp.float32) + jnp.dot(hidden, feedforward_output_weight, preferred_element_type=jnp.float32)).astype(jnp.bfloat16)
```

```python
import math

import jax
import jax.numpy as jnp
from jax import lax
from jax.sharding import Mesh, PartitionSpec as P

H = 12
DH = 64
D = H * DH
GROUPS = 4
HG = H // GROUPS
ROWS = 128
PLANE = ("y_lo", "x", "y_hi")
SEQ = ("y_lo", "x")


def normalize_rows(values_in):
    wide = values_in.astype(jnp.float32)
    centre = jnp.mean(wide, axis=-1, keepdims=True)
    variance = jnp.mean((wide - centre) ** 2, axis=-1, keepdims=True)
    return ((wide - centre) * lax.rsqrt(variance + 1e-05)).astype(jnp.bfloat16)


def dot32(a, b):
    return jnp.dot(a, b, preferred_element_type=jnp.float32)


def per_device(x, row_qkv, row_out, col_qkv, col_out, ff_in, ff_out):
    normed = normalize_rows(x).reshape(2, 256, D)
    by_group = row_qkv.reshape(D, 3, GROUPS, HG * DH).transpose(2, 0, 1, 3).reshape(GROUPS, D, 576)
    proj = jnp.einsum("ytd,zde->yzte", normed, by_group, preferred_element_type=jnp.float32)
    proj = proj.astype(jnp.bfloat16).reshape(8, 256, 576)
    x_cols = x.reshape(16, 8, 4, D).transpose(1, 2, 0, 3)
    x_cols = lax.all_to_all(x_cols, SEQ, 0, 0, tiled=True)
    got = lax.all_to_all(proj, ("y_hi", "z"), 0, 0, tiled=True)
    got = got.reshape(8, 8, 32, 3, HG, DH)
    q, k, v = got[:, :, :, 0], got[:, :, :, 1], got[:, :, :, 2]
    swap = [(0, 1), (1, 0)]
    k2 = lax.ppermute(k, "core", swap)
    v2 = lax.ppermute(v, "core", swap)
    k_all = jnp.stack([k, k2])
    v_all = jnp.stack([v, v2])
    scores = jnp.einsum("arihc,kbrjhc->haikbj", q, k_all, preferred_element_type=jnp.float32)
    scores = scores.reshape(HG, 16, 16, 512).transpose(1, 0, 2, 3).astype(jnp.bfloat16)
    parts = lax.all_to_all(scores, PLANE, 0, 0, tiled=True)
    total = jnp.sum(parts.astype(jnp.float32), axis=0) * (1.0 / math.sqrt(DH * ROWS))
    weights = jax.nn.softmax(total, axis=-1).astype(jnp.bfloat16)
    weights = lax.all_gather(weights, PLANE, axis=0, tiled=False)
    weights = weights.transpose(1, 0, 2, 3).reshape(HG, 8, 32, 2, 8, 32)
    att = jnp.einsum("haikbj,kbrjhc->airhc", weights, v_all, preferred_element_type=jnp.float32)
    att = att.astype(jnp.bfloat16).reshape(8, 8, 4, 8, HG * DH)
    att = att.transpose(1, 0, 2, 3, 4).reshape(64, 4, 8, HG * DH)
    att = lax.all_to_all(att, ("y_lo", "x", "y_hi", "z"), 0, 0, tiled=True)
    att = att.reshape(16, GROUPS, 4, 8, HG * DH).transpose(2, 0, 3, 1, 4).reshape(512, D)
    x_cols = x_cols.transpose(1, 0, 2, 3).reshape(512, D)
    after_rows = (x_cols.astype(jnp.float32) + dot32(att, row_out)).astype(jnp.bfloat16)
    col = dot32(normalize_rows(after_rows), col_qkv).astype(jnp.bfloat16)
    col = col.reshape(4, ROWS, 3, H, DH)
    cq, ck, cv = col[:, :, 0], col[:, :, 1], col[:, :, 2]
    cs = jnp.einsum("jrhc,jshc->jhrs", cq, ck, preferred_element_type=jnp.float32)
    cw = jax.nn.softmax(cs * (1.0 / math.sqrt(DH)), axis=-1).astype(jnp.bfloat16)
    co = jnp.einsum("jhrs,jshc->jrhc", cw, cv, preferred_element_type=jnp.float32)
    co = co.astype(jnp.bfloat16).reshape(512, D)
    after_cols = (after_rows.astype(jnp.float32) + dot32(co, col_out)).astype(jnp.bfloat16)
    hidden = jax.nn.gelu(dot32(normalize_rows(after_cols), ff_in)).astype(jnp.bfloat16)
    out = (after_cols.astype(jnp.float32) + dot32(hidden, ff_out)).astype(jnp.bfloat16)
    out = out.reshape(4, 8, 16, D).transpose(1, 0, 2, 3)
    out = lax.all_to_all(out, SEQ, 0, 0, tiled=True)
    return out.transpose(2, 0, 1, 3).reshape(16, 32, D)


def solution(mesh):
    fine = Mesh(mesh.devices.reshape(2, 4, 2, 4, 2), ("y_lo", "x", "y_hi", "z", "core"))
    tokens = P(SEQ, ("y_hi", "z", "core"), None)
    placed = (tokens, P(), P(), P(), P(), P(), P())
    return jax.shard_map(per_device, mesh=fine, in_specs=placed, out_specs=tokens, check_vma=False)
```

```python
import functools
import math

import jax
import jax.numpy as jnp
from jax import lax
from jax.experimental import pallas as pl
from jax.experimental.pallas import tpu as pltpu
from jax.sharding import Mesh, PartitionSpec as P

H = 12
DH = 64
D = H * DH
FF = 4 * D
ROWS = 128
SEQ = ("y_lo", "x")
PLANE = ("y_lo", "x", "y_hi")
CHIPS = ("y_lo", "x", "y_hi", "z")
BF = jnp.bfloat16
F32 = jnp.float32
MIB = 1 << 20

FULL = (0, 2, 3, 5)
HALF = (1, 1, 4, 4)


def dot32(a, b):
    return jnp.dot(a, b, preferred_element_type=F32)


def dot_t(a, b):
    return lax.dot_general(a, b, (((1,), (1,)), ((), ())), preferred_element_type=F32)


def swap_halves(v):
    return pltpu.roll(v, 64, 1)


def low_lanes(shape):
    return lax.broadcasted_iota(jnp.int32, shape, len(shape) - 1) % 128 < 64


def normalize(wide):
    centre = jnp.mean(wide, axis=-1, keepdims=True)
    off = wide - centre
    variance = jnp.mean(off * off, axis=-1, keepdims=True)
    return (off * lax.rsqrt(variance + 1e-05)).astype(BF)


def params(mib, **kw):
    return pltpu.CompilerParams(vmem_limit_bytes=mib * MIB, **kw)


def project_kernel(x_ref, w_ref, out_ref, normed):
    @pl.when(pl.program_id(0) == 0)
    def _():
        normed[...] = normalize(x_ref[...].astype(F32))

    val = dot32(normed[...], w_ref[...])
    low = low_lanes((128, 128))
    for z in range(4):
        for half in range(2):
            full = val[half * 256 : half * 256 + 256, FULL[z] * 128 : FULL[z] * 128 + 128]
            out_ref[half * 4 + z, 0:256, :] = full.astype(BF)
            cols = slice(HALF[z] * 128, HALF[z] * 128 + 128)
            first = val[half * 256 : half * 256 + 128, cols]
            second = val[half * 256 + 128 : half * 256 + 256, cols]
            if z % 2 == 0:
                pair = jnp.where(low, first, swap_halves(second))
            else:
                pair = jnp.where(low, swap_halves(first), second)
            out_ref[half * 4 + z, 256:384, :] = pair.astype(BF)


def project(x, w):
    return pl.pallas_call(
        project_kernel,
        grid=(3,),
        in_specs=[
            pl.BlockSpec((512, D), lambda t: (0, 0)),
            pl.BlockSpec((D, D), lambda t: (0, t)),
        ],
        out_specs=pl.BlockSpec((8, 384, 128), lambda t: (0, t, 0)),
        out_shape=jax.ShapeDtypeStruct((8, 1152, 128), BF),
        scratch_shapes=[pltpu.VMEM((512, D), BF)],
        compiler_params=params(24),
        cost_estimate=pl.CostEstimate(
            flops=2 * 512 * D * 3 * D, bytes_accessed=6 * MIB, transcendentals=0
        ),
        name="project",
    )(x, w)


def rows_of(ref, start):
    return ref[:, start : start + 32, :].reshape(256, 128)


def scores_kernel(q_ref, k1_ref, k2_ref, out_ref):
    low = low_lanes((256, 256))
    zero = jnp.zeros((256, 256), BF)
    total = [None, None, None]

    def add(h, part):
        total[h] = part if total[h] is None else total[h] + part

    def keys(start):
        return jnp.concatenate([rows_of(k1_ref, start), rows_of(k2_ref, start)], axis=0)

    for start in range(0, 384, 64):
        q = jnp.concatenate([rows_of(q_ref, start), rows_of(q_ref, start + 32)], axis=1)
        k = jnp.concatenate([keys(start), keys(start + 32)], axis=1)
        if start < 256:
            add(0, dot_t(jnp.where(low, q, zero), k))
            add(1, dot_t(jnp.where(low, zero, q), k))
        else:
            add(2, dot_t(q, k))
    for h in range(3):
        out_ref[:, h] = total[h].astype(BF).reshape(16, 16, 512)


def scores(got, k2):
    return pl.pallas_call(
        scores_kernel,
        grid=(1,),
        in_specs=[
            pl.BlockSpec((8, 384, 128), lambda t: (0, 0, 0)),
            pl.BlockSpec((8, 384, 128), lambda t: (0, 1, 0)),
            pl.BlockSpec((8, 384, 128), lambda t: (0, 0, 0)),
        ],
        out_specs=pl.BlockSpec((16, 3, 16, 512), lambda t: (0, 0, 0, 0)),
        out_shape=jax.ShapeDtypeStruct((16, 3, 16, 512), BF),
        compiler_params=params(24),
        cost_estimate=pl.CostEstimate(
            flops=2 * 5 * 256 * 512 * 512, bytes_accessed=3 * MIB, transcendentals=0
        ),
        name="scores",
    )(got, got, k2)


def softmax_kernel(parts_ref, out_ref):
    total = parts_ref[0].astype(F32)
    for s in range(1, 16):
        total += parts_ref[s].astype(F32)
    total *= 1.0 / math.sqrt(DH * ROWS)
    e = jnp.exp(total - jnp.max(total, axis=-1, keepdims=True))
    w = (e / jnp.sum(e, axis=-1, keepdims=True)).astype(BF)
    for s in range(16):
        out_ref[s] = w


def softmax(parts):
    return pl.pallas_call(
        softmax_kernel,
        out_shape=jax.ShapeDtypeStruct((16, 3, 16, 512), BF),
        compiler_params=params(16),
        cost_estimate=pl.CostEstimate(flops=MIB, bytes_accessed=2 * MIB, transcendentals=24576),
        name="softmax",
    )(parts)


def attend_kernel(w_ref, v1_ref, v2_ref, out_ref, full, part):
    low = low_lanes((256, 256))

    def values(start):
        return jnp.concatenate([rows_of(v1_ref, start), rows_of(v2_ref, start)], axis=0)

    weights = [w_ref[:, h].reshape(256, 512) for h in range(3)]
    for r in range(0, 8, 2):
        v = jnp.concatenate([values(r * 32), values(r * 32 + 32)], axis=1)
        got = jnp.where(low, dot32(weights[0], v), dot32(weights[1], v))
        full[pl.ds(r, 256, stride=8), :] = got[:, :128]
        full[pl.ds(r + 1, 256, stride=8), :] = got[:, 128:]
    for r in range(0, 4, 2):
        v = jnp.concatenate([values(256 + r * 32), values(288 + r * 32)], axis=1)
        got = dot32(weights[2], v)
        for s in range(2):
            tile = got[:, s * 128 : s * 128 + 128]
            part[pl.ds(r + s, 256, stride=8), :] = tile
            part[pl.ds(r + s + 4, 256, stride=8), :] = swap_halves(tile)
    low = low_lanes((16, 128))
    for a in range(8):
        for s in range(8):
            at = (a * 8 + s) * 32
            to = s * 8 + a
            out_ref[to, 0:32, :] = full[at : at + 32, :].astype(BF)
            pair = jnp.where(low, part[at : at + 16, :], swap_halves(part[at + 16 : at + 32, :]))
            out_ref[to, 32:48, :] = pair.astype(BF)


def attend(w, got, v2):
    return pl.pallas_call(
        attend_kernel,
        grid=(1,),
        in_specs=[
            pl.BlockSpec((16, 3, 16, 512), lambda t: (0, 0, 0, 0)),
            pl.BlockSpec((8, 384, 128), lambda t: (0, 2, 0)),
            pl.BlockSpec((8, 384, 128), lambda t: (0, 0, 0)),
        ],
        out_specs=pl.BlockSpec((64, 48, 128), lambda t: (0, 0, 0)),
        out_shape=jax.ShapeDtypeStruct((64, 48, 128), BF),
        scratch_shapes=[pltpu.VMEM((2048, 128), F32), pltpu.VMEM((2048, 128), F32)],
        compiler_params=params(24),
        cost_estimate=pl.CostEstimate(
            flops=2 * 5 * 256 * 512 * 512, bytes_accessed=3 * MIB, transcendentals=0
        ),
        name="attend",
    )(w, got, v2)


def columns_kernel(
    att_ref, x_ref, wo_hbm, wqkv_hbm, wco_hbm, w1_hbm, w2_hbm, out_ref,
    wo, wqkv, wco, w1, w2, att, state, col, sems,
):
    copies = []
    for at, (src, dst) in enumerate(
        ((wo_hbm, wo), (wqkv_hbm, wqkv), (wco_hbm, wco), (w1_hbm, w1), (w2_hbm, w2))
    ):
        copies.append(pltpu.make_async_copy(src, dst, sems.at[at]))
        copies[-1].start()
    low = low_lanes((128, 128))
    for z in range(4):
        whole = att_ref[:, z, 0:32, :].astype(F32).reshape(16, 4, 8, 128)
        for i in range(4):
            tile = whole[:, i].reshape(128, 128).astype(BF)
            att[i * 128 : i * 128 + 128, FULL[z] * 128 : FULL[z] * 128 + 128] = tile
    for p in range(2):
        even = att_ref[:, 2 * p, 32:48, :].astype(F32).reshape(16, 2, 8, 128)
        odd = att_ref[:, 2 * p + 1, 32:48, :].astype(F32).reshape(16, 2, 8, 128)
        for i in range(4):
            first = even[:, i % 2].reshape(128, 128)
            second = odd[:, i % 2].reshape(128, 128)
            if i < 2:
                second = swap_halves(second)
            else:
                first = swap_halves(first)
            tile = jnp.where(low, first, second).astype(BF)
            at = HALF[2 * p] * 128
            att[i * 128 : i * 128 + 128, at : at + 128] = tile
    x = jnp.concatenate([x_ref[:, i].reshape(128, D) for i in range(4)], axis=0)
    copies[0].wait()
    after_rows = (x.astype(F32) + dot32(att[...], wo[...])).astype(BF)
    state[...] = after_rows
    normed = normalize(after_rows.astype(F32))
    copies[1].wait()
    for t in range(3):
        col[:, t * D : t * D + D] = dot32(normed, wqkv[:, t * D : t * D + D]).astype(BF)
    zero = jnp.zeros((128, 128), BF)
    for i in range(4):
        rows = slice(i * 128, i * 128 + 128)
        for t in range(6):
            q = col[rows, t * 128 : t * 128 + 128]
            k = col[rows, D + t * 128 : D + t * 128 + 128]
            v = col[rows, 2 * D + t * 128 : 2 * D + t * 128 + 128]
            pair = jnp.concatenate([jnp.where(low, q, zero), jnp.where(low, zero, q)], axis=0)
            s = dot_t(pair, k) * (1.0 / math.sqrt(DH))
            e = jnp.exp(s - jnp.max(s, axis=-1, keepdims=True))
            w = (e / jnp.sum(e, axis=-1, keepdims=True)).astype(BF)
            o = dot32(w, v)
            att[rows, t * 128 : t * 128 + 128] = jnp.where(low, o[:128], o[128:]).astype(BF)
    copies[2].wait()
    after_cols = (state[...].astype(F32) + dot32(att[...], wco[...])).astype(BF)
    state[...] = after_cols
    normed = normalize(after_cols.astype(F32))
    copies[3].wait()
    copies[4].wait()
    total = after_cols.astype(F32)
    for t in range(4):
        hidden = jax.nn.gelu(dot32(normed, w1[:, t * D : t * D + D])).astype(BF)
        total += dot32(hidden, w2[t * D : t * D + D, :])
    out = total.astype(BF)
    for i in range(4):
        out_ref[:, i] = out[i * 128 : i * 128 + 128].reshape(8, 16, D)


def columns(att, x, wo, wqkv, wco, w1, w2):
    vmem = pl.BlockSpec(memory_space=pltpu.VMEM)
    anywhere = pl.BlockSpec(memory_space=pl.ANY)
    return pl.pallas_call(
        columns_kernel,
        in_specs=[vmem, vmem] + [anywhere] * 5,
        out_specs=vmem,
        out_shape=jax.ShapeDtypeStruct((8, 4, 16, D), BF),
        scratch_shapes=[
            pltpu.VMEM((D, D), BF),
            pltpu.VMEM((D, 3 * D), BF),
            pltpu.VMEM((D, D), BF),
            pltpu.VMEM((D, FF), BF),
            pltpu.VMEM((FF, D), BF),
            pltpu.VMEM((512, D), BF),
            pltpu.VMEM((512, D), BF),
            pltpu.VMEM((512, 3 * D), BF),
            pltpu.SemaphoreType.DMA((5,)),
        ],
        compiler_params=params(48),
        cost_estimate=pl.CostEstimate(
            flops=8 * 10**9, bytes_accessed=18 * MIB, transcendentals=3 * MIB
        ),
        name="columns",
    )(att, x, wo, wqkv, wco, w1, w2)


def per_device(x, row_qkv, row_out, col_qkv, col_out, ff_in, ff_out):
    swap = [(0, 1), (1, 0)]
    got = lax.all_to_all(project(x.reshape(512, D), row_qkv), ("y_hi", "z"), 0, 0, tiled=True)
    k2 = lax.ppermute(got[:, 384:768], "core", swap)
    v2 = lax.ppermute(got[:, 768:], "core", swap)
    x_cols = x.reshape(16, 8, 4, D).transpose(1, 2, 0, 3)
    x_cols = lax.all_to_all(x_cols, SEQ, 0, 0, tiled=True)
    parts = lax.all_to_all(scores(got, k2), PLANE, 0, 0, tiled=True)
    weights = lax.all_to_all(softmax(parts), PLANE, 0, 0, tiled=True)
    att = lax.all_to_all(attend(weights, got, v2), CHIPS, 0, 0, tiled=True)
    out = columns(att.reshape(16, 4, 48, 128), x_cols, row_out, col_qkv, col_out, ff_in, ff_out)
    out = lax.all_to_all(out, SEQ, 0, 0, tiled=True)
    return out.transpose(2, 0, 1, 3).reshape(16, 32, D)


def solution(mesh):
    fine = Mesh(mesh.devices.reshape(2, 4, 2, 4, 2), ("y_lo", "x", "y_hi", "z", "core"))
    tokens = P(SEQ, ("y_hi", "z", "core"), None)
    placed = (tokens, P(), P(), P(), P(), P(), P())
    return jax.shard_map(per_device, mesh=fine, in_specs=placed, out_specs=tokens, check_vma=False)
```

```python
import functools
import math

import jax
import jax.numpy as jnp
from jax import lax
from jax.experimental import pallas as pl
from jax.experimental.pallas import tpu as pltpu
from jax.sharding import Mesh, PartitionSpec as P

H = 12
DH = 64
D = H * DH
FF = 4 * D
ROWS = 128
SEQ = ("y_lo", "x")
PLANE = ("y_lo", "x", "y_hi")
CHIPS = ("y_lo", "x", "y_hi", "z")
BF = jnp.bfloat16
F32 = jnp.float32
MIB = 1 << 20

FULL = (0, 2, 3, 5)
HALF = (1, 1, 4, 4)


def dot32(a, b):
    return jnp.dot(a, b, preferred_element_type=F32)


def dot_t(a, b):
    return lax.dot_general(a, b, (((1,), (1,)), ((), ())), preferred_element_type=F32)


def swap_halves(v):
    return pltpu.roll(v, 64, 1)


def low_lanes(shape):
    return lax.broadcasted_iota(jnp.int32, shape, len(shape) - 1) % 128 < 64


def normalize(wide):
    centre = jnp.mean(wide, axis=-1, keepdims=True)
    off = wide - centre
    variance = jnp.mean(off * off, axis=-1, keepdims=True)
    return (off * lax.rsqrt(variance + 1e-05)).astype(BF)


def params(mib, **kw):
    return pltpu.CompilerParams(vmem_limit_bytes=mib * MIB, **kw)


def project_kernel(x_hbm, w_hbm, out_hbm, x_ref, w_ref, out_ref, sems):
    get_x = pltpu.make_async_copy(x_hbm, x_ref, sems.at[3])
    get_x.start()
    get_w = []
    for t in range(3):
        cols = slice(t * D, t * D + D)
        get_w.append(pltpu.make_async_copy(w_hbm.at[:, cols], w_ref.at[:, cols], sems.at[t]))
    get_w[0].start()
    get_x.wait()
    get_w[1].start()
    get_w[2].start()
    normed = normalize(x_ref[...].astype(F32))
    low = low_lanes((128, 128))
    put = []
    for t in range(3):
        get_w[t].wait()
        val = dot32(normed, w_ref[:, t * D : t * D + D])
        at = t * 384
        for z in range(4):
            for half in range(2):
                full = val[half * 256 : half * 256 + 256, FULL[z] * 128 : FULL[z] * 128 + 128]
                out_ref[half * 4 + z, at : at + 256, :] = full.astype(BF)
                cols = slice(HALF[z] * 128, HALF[z] * 128 + 128)
                first = val[half * 256 : half * 256 + 128, cols]
                second = val[half * 256 + 128 : half * 256 + 256, cols]
                if z % 2 == 0:
                    pair = jnp.where(low, first, swap_halves(second))
                else:
                    pair = jnp.where(low, swap_halves(first), second)
                out_ref[half * 4 + z, at + 256 : at + 384, :] = pair.astype(BF)
        part = pl.ds(at, 384)
        put.append(
            pltpu.make_async_copy(out_ref.at[:, part], out_hbm.at[:, part], sems.at[4 + t])
        )
        put[t].start()
    for t in range(3):
        put[t].wait()


def project(x, w):
    hbm = pl.BlockSpec(memory_space=pltpu.HBM)
    return pl.pallas_call(
        project_kernel,
        in_specs=[hbm, hbm],
        out_specs=hbm,
        out_shape=jax.ShapeDtypeStruct((8, 1152, 128), BF),
        scratch_shapes=[
            pltpu.VMEM((512, D), BF),
            pltpu.VMEM((D, 3 * D), BF),
            pltpu.VMEM((8, 1152, 128), BF),
            pltpu.SemaphoreType.DMA((7,)),
        ],
        compiler_params=params(58),
        cost_estimate=pl.CostEstimate(
            flops=2 * 512 * D * 3 * D, bytes_accessed=6 * MIB, transcendentals=0
        ),
        name="project",
    )(x, w)


def rows_of(ref, start):
    return ref[:, start : start + 32, :].reshape(256, 128)


def scores_kernel(q_ref, k1_ref, k2_ref, out_ref):
    low = low_lanes((256, 256))
    zero = jnp.zeros((256, 256), BF)
    total = [None, None, None]

    def add(h, part):
        total[h] = part if total[h] is None else total[h] + part

    def keys(start):
        return jnp.concatenate([rows_of(k1_ref, start), rows_of(k2_ref, start)], axis=0)

    for start in range(0, 384, 64):
        q = jnp.concatenate([rows_of(q_ref, start), rows_of(q_ref, start + 32)], axis=1)
        k = jnp.concatenate([keys(start), keys(start + 32)], axis=1)
        if start < 256:
            add(0, dot_t(jnp.where(low, q, zero), k))
            add(1, dot_t(jnp.where(low, zero, q), k))
        else:
            add(2, dot_t(q, k))
    for h in range(3):
        out_ref[:, h] = total[h].astype(BF).reshape(16, 16, 512)


def scores(got, k2):
    return pl.pallas_call(
        scores_kernel,
        grid=(1,),
        in_specs=[
            pl.BlockSpec((8, 384, 128), lambda t: (0, 0, 0)),
            pl.BlockSpec((8, 384, 128), lambda t: (0, 1, 0)),
            pl.BlockSpec((8, 384, 128), lambda t: (0, 0, 0)),
        ],
        out_specs=pl.BlockSpec((16, 3, 16, 512), lambda t: (0, 0, 0, 0)),
        out_shape=jax.ShapeDtypeStruct((16, 3, 16, 512), BF),
        compiler_params=params(12),
        cost_estimate=pl.CostEstimate(
            flops=2 * 5 * 256 * 512 * 512, bytes_accessed=3 * MIB, transcendentals=0
        ),
        name="scores",
    )(got, got, k2)


def softmax_kernel(parts_ref, out_ref):
    total = parts_ref[0].astype(F32)
    for s in range(1, 16):
        total += parts_ref[s].astype(F32)
    total *= 1.0 / math.sqrt(DH * ROWS)
    e = jnp.exp(total - jnp.max(total, axis=-1, keepdims=True))
    w = (e / jnp.sum(e, axis=-1, keepdims=True)).astype(BF)
    for s in range(16):
        out_ref[s] = w


def softmax(parts):
    return pl.pallas_call(
        softmax_kernel,
        out_shape=jax.ShapeDtypeStruct((16, 3, 16, 512), BF),
        compiler_params=params(6),
        cost_estimate=pl.CostEstimate(flops=MIB, bytes_accessed=2 * MIB, transcendentals=24576),
        name="softmax",
    )(parts)


def attend_kernel(w_ref, v1_ref, v2_ref, out_ref, full, part):
    low = low_lanes((256, 256))

    def values(start):
        return jnp.concatenate([rows_of(v1_ref, start), rows_of(v2_ref, start)], axis=0)

    weights = [w_ref[:, h].reshape(256, 512) for h in range(3)]
    for r in range(0, 8, 2):
        v = jnp.concatenate([values(r * 32), values(r * 32 + 32)], axis=1)
        got = jnp.where(low, dot32(weights[0], v), dot32(weights[1], v))
        full[pl.ds(r, 256, stride=8), :] = got[:, :128]
        full[pl.ds(r + 1, 256, stride=8), :] = got[:, 128:]
    for r in range(0, 4, 2):
        v = jnp.concatenate([values(256 + r * 32), values(288 + r * 32)], axis=1)
        got = dot32(weights[2], v)
        for s in range(2):
            tile = got[:, s * 128 : s * 128 + 128]
            part[pl.ds(r + s, 256, stride=8), :] = tile
            part[pl.ds(r + s + 4, 256, stride=8), :] = swap_halves(tile)
    low = low_lanes((16, 128))
    for a in range(8):
        for s in range(8):
            at = (a * 8 + s) * 32
            to = s * 8 + a
            out_ref[to, 0:32, :] = full[at : at + 32, :].astype(BF)
            pair = jnp.where(low, part[at : at + 16, :], swap_halves(part[at + 16 : at + 32, :]))
            out_ref[to, 32:48, :] = pair.astype(BF)


def attend(w, got, v2):
    return pl.pallas_call(
        attend_kernel,
        grid=(1,),
        in_specs=[
            pl.BlockSpec((16, 3, 16, 512), lambda t: (0, 0, 0, 0)),
            pl.BlockSpec((8, 384, 128), lambda t: (0, 2, 0)),
            pl.BlockSpec((8, 384, 128), lambda t: (0, 0, 0)),
        ],
        out_specs=pl.BlockSpec((64, 48, 128), lambda t: (0, 0, 0)),
        out_shape=jax.ShapeDtypeStruct((64, 48, 128), BF),
        scratch_shapes=[pltpu.VMEM((2048, 128), F32), pltpu.VMEM((2048, 128), F32)],
        compiler_params=params(12),
        cost_estimate=pl.CostEstimate(
            flops=2 * 5 * 256 * 512 * 512, bytes_accessed=3 * MIB, transcendentals=0
        ),
        name="attend",
    )(w, got, v2)


def columns_kernel(
    me_ref, att_hbm, x0, x1, x2, x3, wo_hbm, wqkv_hbm, wco_hbm, w1_hbm, w2_hbm, out_ref,
    att_ref, wo, wqkv, wco, w1, w2, att, x_in, state, col, sems,
):
    def copy(src, dst, sem):
        return pltpu.make_async_copy(src, dst, sems.at[sem])

    get_att = copy(att_hbm, att_ref, 0)
    get_att.start()
    get_wo = copy(wo_hbm, wo, 1)
    get_wo.start()
    get_x = []
    for k, block in enumerate((x0, x1, x2, x3)):
        for side in range(2):
            y = me_ref[0] if side == 0 else 1 - me_ref[0]
            at = pl.multiple_of((y * 4 + (me_ref[1] ^ k)) * 16, 16)
            get_x.append(copy(block.at[side], x_in.at[:, pl.ds(at, 16), :], 2 + 2 * k + side))
            get_x[-1].start()
    get_wqkv = copy(wqkv_hbm, wqkv, 10)
    get_wqkv.start()
    get_wco = copy(wco_hbm, wco, 11)
    get_w1 = copy(w1_hbm, w1, 12)
    get_w2 = copy(w2_hbm, w2, 13)
    get_att.wait()
    low = low_lanes((128, 128))
    for z in range(4):
        whole = att_ref[:, z, 0:32, :].astype(F32).reshape(16, 4, 8, 128)
        for i in range(4):
            tile = whole[:, i].reshape(128, 128).astype(BF)
            att[i * 128 : i * 128 + 128, FULL[z] * 128 : FULL[z] * 128 + 128] = tile
    for p in range(2):
        even = att_ref[:, 2 * p, 32:48, :].astype(F32).reshape(16, 2, 8, 128)
        odd = att_ref[:, 2 * p + 1, 32:48, :].astype(F32).reshape(16, 2, 8, 128)
        for i in range(4):
            first = even[:, i % 2].reshape(128, 128)
            second = odd[:, i % 2].reshape(128, 128)
            if i < 2:
                second = swap_halves(second)
            else:
                first = swap_halves(first)
            tile = jnp.where(low, first, second).astype(BF)
            at = HALF[2 * p] * 128
            att[i * 128 : i * 128 + 128, at : at + 128] = tile
    get_wo.wait()
    for block in get_x:
        block.wait()
    after_rows = (x_in[...].reshape(512, D).astype(F32) + dot32(att[...], wo[...])).astype(BF)
    state[...] = after_rows
    normed = normalize(after_rows.astype(F32))
    get_wqkv.wait()
    get_wco.start()
    get_w1.start()
    get_w2.start()
    for t in range(3):
        col[:, t * D : t * D + D] = dot32(normed, wqkv[:, t * D : t * D + D]).astype(BF)
    zero = jnp.zeros((128, 128), BF)
    for i in range(4):
        rows = slice(i * 128, i * 128 + 128)
        for t in range(6):
            q = col[rows, t * 128 : t * 128 + 128]
            k = col[rows, D + t * 128 : D + t * 128 + 128]
            v = col[rows, 2 * D + t * 128 : 2 * D + t * 128 + 128]
            pair = jnp.concatenate([jnp.where(low, q, zero), jnp.where(low, zero, q)], axis=0)
            s = dot_t(pair, k) * (1.0 / math.sqrt(DH))
            e = jnp.exp(s - jnp.max(s, axis=-1, keepdims=True))
            w = (e / jnp.sum(e, axis=-1, keepdims=True)).astype(BF)
            o = dot32(w, v)
            att[rows, t * 128 : t * 128 + 128] = jnp.where(low, o[:128], o[128:]).astype(BF)
    get_wco.wait()
    after_cols = (state[...].astype(F32) + dot32(att[...], wco[...])).astype(BF)
    state[...] = after_cols
    normed = normalize(after_cols.astype(F32))
    get_w1.wait()
    get_w2.wait()
    total = after_cols.astype(F32)
    for t in range(4):
        hidden = jax.nn.gelu(dot32(normed, w1[:, t * D : t * D + D])).astype(BF)
        total += dot32(hidden, w2[t * D : t * D + D, :])
    out = total.astype(BF)
    for i in range(4):
        out_ref[:, i] = out[i * 128 : i * 128 + 128].reshape(8, 16, D)


def columns(me, att, x, wo, wqkv, wco, w1, w2):
    vmem = pl.BlockSpec(memory_space=pltpu.VMEM)
    anywhere = pl.BlockSpec(memory_space=pl.ANY)
    return pl.pallas_call(
        columns_kernel,
        in_specs=[pl.BlockSpec(memory_space=pltpu.SMEM)] + [anywhere] * 10,
        out_specs=vmem,
        out_shape=jax.ShapeDtypeStruct((8, 4, 16, D), BF),
        scratch_shapes=[
            pltpu.VMEM((16, 4, 48, 128), BF),
            pltpu.VMEM((D, D), BF),
            pltpu.VMEM((D, 3 * D), BF),
            pltpu.VMEM((D, D), BF),
            pltpu.VMEM((D, FF), BF),
            pltpu.VMEM((FF, D), BF),
            pltpu.VMEM((512, D), BF),
            pltpu.VMEM((4, 128, D), BF),
            pltpu.VMEM((512, D), BF),
            pltpu.VMEM((512, 3 * D), BF),
            pltpu.SemaphoreType.DMA((14,)),
        ],
        compiler_params=params(60),
        cost_estimate=pl.CostEstimate(
            flops=8 * 10**9, bytes_accessed=18 * MIB, transcendentals=3 * MIB
        ),
        name="columns",
    )(me, att, *x, wo, wqkv, wco, w1, w2)


def per_device(x, row_qkv, row_out, col_qkv, col_out, ff_in, ff_out):
    barrier = lax.optimization_barrier
    swap = [(0, 1), (1, 0)]
    y_me, x_me = lax.axis_index("y_lo"), lax.axis_index("x")
    halves = x.reshape(16, 2, 16, D)
    far = lax.ppermute(lax.dynamic_index_in_dim(halves, 1 - y_me, 1, False), "y_lo", swap)
    proj, x, far = barrier((project(x.reshape(512, D), row_qkv), x, far))
    got = lax.all_to_all(proj, ("y_hi", "z"), 0, 0, tiled=True)
    mine = lax.dynamic_index_in_dim(x.reshape(16, 2, 16, D), y_me, 1, False)
    x_cols = jnp.stack([mine, far]).reshape(2, 16, 4, 4, D).transpose(2, 0, 3, 1, 4)
    near = []
    for k in range(4):
        block = lax.dynamic_index_in_dim(x_cols, x_me ^ k, 0, False)
        near.append(lax.ppermute(block, "x", [(i, i ^ k) for i in range(4)]) if k else block)
    got, near = barrier((got, near))
    k2 = lax.ppermute(got[:, 384:768], "core", swap)
    parts, got = barrier((scores(got, k2), got))
    parts = lax.all_to_all(parts, PLANE, 0, 0, tiled=True)
    v2 = lax.ppermute(got[:, 768:], "core", swap)
    parts, v2 = barrier((parts, v2))
    shares = lax.all_to_all(softmax(parts), PLANE, 0, 0, tiled=True)
    att = lax.all_to_all(attend(shares, got, v2), CHIPS, 0, 0, tiled=True)
    att = att.reshape(16, 4, 48, 128)
    me = jnp.stack([y_me, x_me]).astype(jnp.int32)
    out = columns(me, att, near, row_out, col_qkv, col_out, ff_in, ff_out)
    out = lax.all_to_all(out, SEQ, 0, 0, tiled=True)
    return out.transpose(2, 0, 1, 3).reshape(16, 32, D)


def solution(mesh):
    fine = Mesh(mesh.devices.reshape(2, 4, 2, 4, 2), ("y_lo", "x", "y_hi", "z", "core"))
    tokens = P(SEQ, ("y_hi", "z", "core"), None)
    placed = (tokens, P(), P(), P(), P(), P(), P())
    return jax.shard_map(per_device, mesh=fine, in_specs=placed, out_specs=tokens, check_vma=False)
```

```python
import functools
import math

import jax
import jax.numpy as jnp
from jax import lax
from jax.experimental import pallas as pl
from jax.experimental.pallas import tpu as pltpu
from jax.sharding import Mesh, PartitionSpec as P

H = 12
DH = 64
D = H * DH
FF = 4 * D
ROWS = 128
SEQ = ("y_lo", "x")
PLANE = ("y_lo", "x", "y_hi")
CHIPS = ("y_lo", "x", "y_hi", "z")
BF = jnp.bfloat16
F32 = jnp.float32
MIB = 1 << 20

FULL = (0, 2, 3, 5)
HALF = (1, 1, 4, 4)


def dot32(a, b):
    return jnp.dot(a, b, preferred_element_type=F32)


def dot_t(a, b):
    return lax.dot_general(a, b, (((1,), (1,)), ((), ())), preferred_element_type=F32)


def swap_halves(v):
    return pltpu.roll(v, 64, 1)


def low_lanes(shape):
    return lax.broadcasted_iota(jnp.int32, shape, len(shape) - 1) % 128 < 64


def normalize(wide):
    centre = jnp.mean(wide, axis=-1, keepdims=True)
    off = wide - centre
    variance = jnp.mean(off * off, axis=-1, keepdims=True)
    return (off * lax.rsqrt(variance + 1e-05)).astype(BF)


def params(mib, **kw):
    return pltpu.CompilerParams(vmem_limit_bytes=mib * MIB, **kw)


def project_kernel(x_hbm, w_hbm, out_hbm, x_ref, w_ref, out_ref, sems):
    get_x = pltpu.make_async_copy(x_hbm, x_ref, sems.at[3])
    get_x.start()
    get_w = []
    for t in range(3):
        cols = slice(t * D, t * D + D)
        get_w.append(pltpu.make_async_copy(w_hbm.at[:, cols], w_ref.at[:, cols], sems.at[t]))
    get_w[0].start()
    get_x.wait()
    get_w[1].start()
    get_w[2].start()
    normed = normalize(x_ref[...].astype(F32))
    low = low_lanes((128, 128))
    put = []
    for t in range(3):
        get_w[t].wait()
        val = dot32(normed, w_ref[:, t * D : t * D + D])
        at = t * 384
        for z in range(4):
            for half in range(2):
                full = val[half * 256 : half * 256 + 256, FULL[z] * 128 : FULL[z] * 128 + 128]
                out_ref[half * 4 + z, at : at + 256, :] = full.astype(BF)
                cols = slice(HALF[z] * 128, HALF[z] * 128 + 128)
                first = val[half * 256 : half * 256 + 128, cols]
                second = val[half * 256 + 128 : half * 256 + 256, cols]
                if z % 2 == 0:
                    pair = jnp.where(low, first, swap_halves(second))
                else:
                    pair = jnp.where(low, swap_halves(first), second)
                out_ref[half * 4 + z, at + 256 : at + 384, :] = pair.astype(BF)
        part = pl.ds(at, 384)
        put.append(
            pltpu.make_async_copy(out_ref.at[:, part], out_hbm.at[:, part], sems.at[4 + t])
        )
        put[t].start()
    for t in range(3):
        put[t].wait()


def project(x, w):
    hbm = pl.BlockSpec(memory_space=pltpu.HBM)
    return pl.pallas_call(
        project_kernel,
        in_specs=[hbm, hbm],
        out_specs=hbm,
        out_shape=jax.ShapeDtypeStruct((8, 1152, 128), BF),
        scratch_shapes=[
            pltpu.VMEM((512, D), BF),
            pltpu.VMEM((D, 3 * D), BF),
            pltpu.VMEM((8, 1152, 128), BF),
            pltpu.SemaphoreType.DMA((7,)),
        ],
        compiler_params=params(58),
        cost_estimate=pl.CostEstimate(
            flops=2 * 512 * D * 3 * D, bytes_accessed=6 * MIB, transcendentals=0
        ),
        name="project",
    )(x, w)


def rows_of(ref, start):
    return ref[:, start : start + 32, :].reshape(256, 128)


def scores_kernel(q_ref, k1_ref, k2_ref, out_ref):
    low = low_lanes((256, 256))
    zero = jnp.zeros((256, 256), BF)
    total = [None, None, None]

    def add(h, part):
        total[h] = part if total[h] is None else total[h] + part

    def keys(start):
        return jnp.concatenate([rows_of(k1_ref, start), rows_of(k2_ref, start)], axis=0)

    for start in range(0, 384, 64):
        q = jnp.concatenate([rows_of(q_ref, start), rows_of(q_ref, start + 32)], axis=1)
        k = jnp.concatenate([keys(start), keys(start + 32)], axis=1)
        if start < 256:
            add(0, dot_t(jnp.where(low, q, zero), k))
            add(1, dot_t(jnp.where(low, zero, q), k))
        else:
            add(2, dot_t(q, k))
    for h in range(3):
        out_ref[:, h] = total[h].astype(BF).reshape(16, 16, 512)


def scores(got, k2):
    return pl.pallas_call(
        scores_kernel,
        grid=(1,),
        in_specs=[
            pl.BlockSpec((8, 384, 128), lambda t: (0, 0, 0)),
            pl.BlockSpec((8, 384, 128), lambda t: (0, 1, 0)),
            pl.BlockSpec((8, 384, 128), lambda t: (0, 0, 0)),
        ],
        out_specs=pl.BlockSpec((16, 3, 16, 512), lambda t: (0, 0, 0, 0)),
        out_shape=jax.ShapeDtypeStruct((16, 3, 16, 512), BF),
        compiler_params=params(12),
        cost_estimate=pl.CostEstimate(
            flops=2 * 5 * 256 * 512 * 512, bytes_accessed=3 * MIB, transcendentals=0
        ),
        name="scores",
    )(got, got, k2)


def softmax_kernel(parts_ref, out_ref):
    total = parts_ref[0].astype(F32)
    for s in range(1, 16):
        total += parts_ref[s].astype(F32)
    total *= 1.0 / math.sqrt(DH * ROWS)
    e = jnp.exp(total - jnp.max(total, axis=-1, keepdims=True))
    w = (e / jnp.sum(e, axis=-1, keepdims=True)).astype(BF)
    for s in range(16):
        out_ref[s] = w


def softmax(parts):
    return pl.pallas_call(
        softmax_kernel,
        out_shape=jax.ShapeDtypeStruct((16, 3, 16, 512), BF),
        compiler_params=params(6),
        cost_estimate=pl.CostEstimate(flops=MIB, bytes_accessed=2 * MIB, transcendentals=24576),
        name="softmax",
    )(parts)


def attend_kernel(w_ref, v1_ref, v2_ref, out_ref, full, part):
    low = low_lanes((256, 256))

    def values(start):
        return jnp.concatenate([rows_of(v1_ref, start), rows_of(v2_ref, start)], axis=0)

    weights = [w_ref[:, h].reshape(256, 512) for h in range(3)]
    for r in range(0, 8, 2):
        v = jnp.concatenate([values(r * 32), values(r * 32 + 32)], axis=1)
        got = jnp.where(low, dot32(weights[0], v), dot32(weights[1], v))
        full[pl.ds(r, 256, stride=8), :] = got[:, :128]
        full[pl.ds(r + 1, 256, stride=8), :] = got[:, 128:]
    for r in range(0, 4, 2):
        v = jnp.concatenate([values(256 + r * 32), values(288 + r * 32)], axis=1)
        got = dot32(weights[2], v)
        for s in range(2):
            tile = got[:, s * 128 : s * 128 + 128]
            part[pl.ds(r + s, 256, stride=8), :] = tile
            part[pl.ds(r + s + 4, 256, stride=8), :] = swap_halves(tile)
    low = low_lanes((16, 128))
    for a in range(8):
        for s in range(8):
            at = (a * 8 + s) * 32
            to = s * 8 + a
            out_ref[to, 0:32, :] = full[at : at + 32, :].astype(BF)
            pair = jnp.where(low, part[at : at + 16, :], swap_halves(part[at + 16 : at + 32, :]))
            out_ref[to, 32:48, :] = pair.astype(BF)


def attend(w, got, v2):
    return pl.pallas_call(
        attend_kernel,
        grid=(1,),
        in_specs=[
            pl.BlockSpec((16, 3, 16, 512), lambda t: (0, 0, 0, 0)),
            pl.BlockSpec((8, 384, 128), lambda t: (0, 2, 0)),
            pl.BlockSpec((8, 384, 128), lambda t: (0, 0, 0)),
        ],
        out_specs=pl.BlockSpec((64, 48, 128), lambda t: (0, 0, 0)),
        out_shape=jax.ShapeDtypeStruct((64, 48, 128), BF),
        scratch_shapes=[pltpu.VMEM((2048, 128), F32), pltpu.VMEM((2048, 128), F32)],
        compiler_params=params(12),
        cost_estimate=pl.CostEstimate(
            flops=2 * 5 * 256 * 512 * 512, bytes_accessed=3 * MIB, transcendentals=0
        ),
        name="attend",
    )(w, got, v2)


def columns_kernel(
    me_ref, att_ref, x0, x1, x2, x3, wo, wqkv, wco, w1, w2, out_ref,
    att, x_in, state, col, sems,
):
    def copy(src, dst, sem):
        return pltpu.make_async_copy(src, dst, sems.at[sem])

    get_x = []
    for k, block in enumerate((x0, x1, x2, x3)):
        for side in range(2):
            y = me_ref[0] if side == 0 else 1 - me_ref[0]
            at = pl.multiple_of((y * 4 + (me_ref[1] ^ k)) * 16, 16)
            get_x.append(copy(block.at[side], x_in.at[:, pl.ds(at, 16), :], 2 + 2 * k + side))
            get_x[-1].start()
    low = low_lanes((128, 128))
    for z in range(4):
        whole = att_ref[:, z, 0:32, :].astype(F32).reshape(16, 4, 8, 128)
        for i in range(4):
            tile = whole[:, i].reshape(128, 128).astype(BF)
            att[i * 128 : i * 128 + 128, FULL[z] * 128 : FULL[z] * 128 + 128] = tile
    for p in range(2):
        even = att_ref[:, 2 * p, 32:48, :].astype(F32).reshape(16, 2, 8, 128)
        odd = att_ref[:, 2 * p + 1, 32:48, :].astype(F32).reshape(16, 2, 8, 128)
        for i in range(4):
            first = even[:, i % 2].reshape(128, 128)
            second = odd[:, i % 2].reshape(128, 128)
            if i < 2:
                second = swap_halves(second)
            else:
                first = swap_halves(first)
            tile = jnp.where(low, first, second).astype(BF)
            at = HALF[2 * p] * 128
            att[i * 128 : i * 128 + 128, at : at + 128] = tile
    for block in get_x:
        block.wait()
    after_rows = (x_in[...].reshape(512, D).astype(F32) + dot32(att[...], wo[...])).astype(BF)
    state[...] = after_rows
    normed = normalize(after_rows.astype(F32))
    for t in range(3):
        col[:, t * D : t * D + D] = dot32(normed, wqkv[:, t * D : t * D + D]).astype(BF)
    zero = jnp.zeros((128, 128), BF)
    for i in range(4):
        rows = slice(i * 128, i * 128 + 128)
        for t in range(6):
            q = col[rows, t * 128 : t * 128 + 128]
            k = col[rows, D + t * 128 : D + t * 128 + 128]
            v = col[rows, 2 * D + t * 128 : 2 * D + t * 128 + 128]
            pair = jnp.concatenate([jnp.where(low, q, zero), jnp.where(low, zero, q)], axis=0)
            s = dot_t(pair, k) * (1.0 / math.sqrt(DH))
            e = jnp.exp(s - jnp.max(s, axis=-1, keepdims=True))
            w = (e / jnp.sum(e, axis=-1, keepdims=True)).astype(BF)
            o = dot32(w, v)
            att[rows, t * 128 : t * 128 + 128] = jnp.where(low, o[:128], o[128:]).astype(BF)
    after_cols = (state[...].astype(F32) + dot32(att[...], wco[...])).astype(BF)
    state[...] = after_cols
    normed = normalize(after_cols.astype(F32))
    total = after_cols.astype(F32)
    for t in range(4):
        hidden = jax.nn.gelu(dot32(normed, w1[:, t * D : t * D + D])).astype(BF)
        total += dot32(hidden, w2[t * D : t * D + D, :])
    out = total.astype(BF)
    for i in range(4):
        out_ref[:, i] = out[i * 128 : i * 128 + 128].reshape(8, 16, D)


def columns(me, att, x, wo, wqkv, wco, w1, w2):
    vmem = pl.BlockSpec(memory_space=pltpu.VMEM)
    anywhere = pl.BlockSpec(memory_space=pl.ANY)
    return pl.pallas_call(
        columns_kernel,
        in_specs=[pl.BlockSpec(memory_space=pltpu.SMEM), vmem]
        + [anywhere] * 4
        + [vmem] * 5,
        out_specs=vmem,
        out_shape=jax.ShapeDtypeStruct((8, 4, 16, D), BF),
        scratch_shapes=[
            pltpu.VMEM((512, D), BF),
            pltpu.VMEM((4, 128, D), BF),
            pltpu.VMEM((512, D), BF),
            pltpu.VMEM((512, 3 * D), BF),
            pltpu.SemaphoreType.DMA((11,)),
        ],
        compiler_params=params(24),
        cost_estimate=pl.CostEstimate(
            flops=8 * 10**9, bytes_accessed=18 * MIB, transcendentals=3 * MIB
        ),
        name="columns",
    )(me, att, *x, wo, wqkv, wco, w1, w2)


def per_device(x, row_qkv, row_out, col_qkv, col_out, ff_in, ff_out):
    barrier = lax.optimization_barrier
    swap = [(0, 1), (1, 0)]
    y_me, x_me = lax.axis_index("y_lo"), lax.axis_index("x")
    halves = x.reshape(16, 2, 16, D)
    far = lax.ppermute(lax.dynamic_index_in_dim(halves, 1 - y_me, 1, False), "y_lo", swap)
    me = jnp.stack([y_me, x_me]).astype(jnp.int32)
    proj, x, far, me = barrier((project(x.reshape(512, D), row_qkv), x, far, me))
    got = lax.all_to_all(proj, ("y_hi", "z"), 0, 0, tiled=True)
    mine = lax.dynamic_index_in_dim(x.reshape(16, 2, 16, D), y_me, 1, False)
    x_cols = jnp.stack([mine, far]).reshape(2, 16, 4, 4, D).transpose(2, 0, 3, 1, 4)
    near = []
    for k in range(4):
        block = lax.dynamic_index_in_dim(x_cols, x_me ^ k, 0, False)
        near.append(lax.ppermute(block, "x", [(i, i ^ k) for i in range(4)]) if k else block)
    got, near = barrier((got, near))
    k2 = lax.ppermute(got[:, 384:768], "core", swap)
    parts, got = barrier((scores(got, k2), got))
    parts = lax.all_to_all(parts, PLANE, 0, 0, tiled=True)
    v2 = lax.ppermute(got[:, 768:], "core", swap)
    parts, v2 = barrier((parts, v2))
    shares = lax.all_to_all(softmax(parts), PLANE, 0, 0, tiled=True)
    att = lax.all_to_all(attend(shares, got, v2), CHIPS, 0, 0, tiled=True)
    att = att.reshape(16, 4, 48, 128)
    out = columns(me, att, near, row_out, col_qkv, col_out, ff_in, ff_out)
    out = lax.all_to_all(out, SEQ, 0, 0, tiled=True)
    return out.transpose(2, 0, 1, 3).reshape(16, 32, D)


def solution(mesh):
    fine = Mesh(mesh.devices.reshape(2, 4, 2, 4, 2), ("y_lo", "x", "y_hi", "z", "core"))
    tokens = P(SEQ, ("y_hi", "z", "core"), None)
    placed = (tokens, P(), P(), P(), P(), P(), P())
    return jax.shard_map(per_device, mesh=fine, in_specs=placed, out_specs=tokens, check_vma=False)
```

```python
import functools
import math

import jax
import jax.numpy as jnp
from jax import lax
from jax.experimental import pallas as pl
from jax.experimental.pallas import tpu as pltpu
from jax.sharding import Mesh, PartitionSpec as P

H = 12
DH = 64
D = H * DH
FF = 4 * D
ROWS = 128
SEQ = ("y_lo", "x")
CHIPS = ("y_lo", "x", "y_hi", "z")
BF = jnp.bfloat16
F32 = jnp.float32
MIB = 1 << 20

FULL = (0, 2, 3, 5)
HALF = (1, 1, 4, 4)

KEY, VALUE, QUERY = 0, 512, 1024


def dot32(a, b):
    return jnp.dot(a, b, preferred_element_type=F32)


def dot_t(a, b):
    return lax.dot_general(a, b, (((1,), (1,)), ((), ())), preferred_element_type=F32)


def swap_halves(v):
    return pltpu.roll(v, 64, 1)


def low_lanes(shape):
    return lax.broadcasted_iota(jnp.int32, shape, len(shape) - 1) % 128 < 64


def normalize(wide):
    centre = jnp.mean(wide, axis=-1, keepdims=True)
    off = wide - centre
    variance = jnp.mean(off * off, axis=-1, keepdims=True)
    return (off * lax.rsqrt(variance + 1e-05)).astype(BF)


def params(mib, **kw):
    return pltpu.CompilerParams(vmem_limit_bytes=mib * MIB, **kw)


def project_kernel(x_hbm, w_hbm, out_hbm, x_ref, w_ref, out_ref, sems):
    get_x = pltpu.make_async_copy(x_hbm, x_ref, sems.at[3])
    get_x.start()
    get_w = []
    for t in range(3):
        cols = slice(t * D, t * D + D)
        get_w.append(pltpu.make_async_copy(w_hbm.at[:, cols], w_ref.at[:, cols], sems.at[t]))
    get_w[0].start()
    get_x.wait()
    get_w[1].start()
    get_w[2].start()
    normed = normalize(x_ref[...].astype(F32))
    low = low_lanes((256, 128))
    put = []
    for t in range(3):
        get_w[t].wait()
        val = dot32(normed, w_ref[:, t * D : t * D + D])
        at = (QUERY, KEY, VALUE)[t]
        for tile in range(6):
            first = val[:256, tile * 128 : tile * 128 + 128]
            second = val[256:, tile * 128 : tile * 128 + 128]
            heads = (
                jnp.where(low, first, swap_halves(second)).astype(BF),
                jnp.where(low, swap_halves(first), second).astype(BF),
            )
            if tile in FULL:
                for y in range(2):
                    out_ref[y * 4 + FULL.index(tile), at : at + 256, :] = heads[y]
            else:
                for y in range(2):
                    for side in range(2):
                        z = HALF.index(tile) + side
                        if t > 0:
                            out_ref[y * 4 + z, at + 256 : at + 512, :] = heads[side]
                        else:
                            part = heads[side].reshape(8, 2, 16, 128)[:, y].reshape(128, 128)
                            out_ref[y * 4 + z, at + 256 : at + 384, :] = part
        part = pl.ds(at, 384 if t == 0 else 512)
        put.append(
            pltpu.make_async_copy(out_ref.at[:, part], out_hbm.at[:, part], sems.at[4 + t])
        )
        put[t].start()
    for t in range(3):
        put[t].wait()


def project(x, w):
    hbm = pl.BlockSpec(memory_space=pltpu.HBM)
    return pl.pallas_call(
        project_kernel,
        in_specs=[hbm, hbm],
        out_specs=hbm,
        out_shape=jax.ShapeDtypeStruct((8, 1408, 128), BF),
        scratch_shapes=[
            pltpu.VMEM((512, D), BF),
            pltpu.VMEM((D, 3 * D), BF),
            pltpu.VMEM((8, 1408, 128), BF),
            pltpu.SemaphoreType.DMA((7,)),
        ],
        compiler_params=params(58),
        cost_estimate=pl.CostEstimate(
            flops=2 * 512 * D * 3 * D, bytes_accessed=6 * MIB, transcendentals=0
        ),
        name="project",
    )(x, w)


def rows_of(ref, start, size=32):
    return ref[:, start : start + size, :].reshape(8 * size, 128)


def pair_of(refs, start):
    sides = [
        jnp.concatenate([rows_of(ref, at + start + 32 * n) for ref, at in refs], axis=0)
        for n in range(2)
    ]
    return jnp.concatenate(sides, axis=1)


def scores_kernel(got_ref, k2_ref, out_ref):
    for head, size in ((0, 32), (1, 16)):
        total = None
        keys = ((got_ref, KEY + head * 256), (k2_ref, head * 256))
        for r in range(0, 8, 2):
            at = QUERY + head * 256 + r * size
            q = jnp.concatenate(
                [rows_of(got_ref, at, size), rows_of(got_ref, at + size, size)], axis=1
            )
            part = dot_t(q, pair_of(keys, r * 32))
            total = part if total is None else total + part
        at = head * 32
        out_ref[:, at : at + size, :] = total.astype(BF).reshape(8, size, 512)


def scores(got, k2):
    vmem = pl.BlockSpec(memory_space=pltpu.VMEM)
    return pl.pallas_call(
        scores_kernel,
        in_specs=[vmem, vmem],
        out_specs=vmem,
        out_shape=jax.ShapeDtypeStruct((8, 48, 512), BF),
        compiler_params=params(12),
        cost_estimate=pl.CostEstimate(
            flops=2 * 384 * 512 * 1024, bytes_accessed=3 * MIB, transcendentals=0
        ),
        name="scores",
    )(got, k2)


def softmax_kernel(parts_ref, out_ref):
    total = parts_ref[0].astype(F32)
    for s in range(1, 8):
        total += parts_ref[s].astype(F32)
    total *= 1.0 / math.sqrt(DH * ROWS)
    e = jnp.exp(total - jnp.max(total, axis=-1, keepdims=True))
    w = (e / jnp.sum(e, axis=-1, keepdims=True)).astype(BF)
    for s in range(8):
        out_ref[s] = w


def softmax(parts):
    return pl.pallas_call(
        softmax_kernel,
        out_shape=jax.ShapeDtypeStruct((8, 48, 512), BF),
        compiler_params=params(6),
        cost_estimate=pl.CostEstimate(flops=MIB, bytes_accessed=MIB, transcendentals=24576),
        name="softmax",
    )(parts)


def attend_kernel(w_ref, got_ref, v2_ref, out_ref, whole, part):
    for head, size, dest in ((0, 32, whole), (1, 16, part)):
        at = head * 32
        w = w_ref[:, at : at + size, :].reshape(8 * size, 512)
        values = ((got_ref, VALUE + head * 256), (v2_ref, head * 256))
        for r in range(0, 8, 2):
            got = dot32(w, pair_of(values, r * 32))
            dest[pl.ds(r, 8 * size, stride=8), :] = got[:, :128]
            dest[pl.ds(r + 1, 8 * size, stride=8), :] = got[:, 128:]
    for a in range(8):
        for s in range(8):
            to = s * 8 + a
            at = (a * 32 + s * 2) * 8
            out_ref[to, 0:16, :] = whole[at : at + 16, :].astype(BF)
            out_ref[to, 16:32, :] = whole[at + 128 : at + 144, :].astype(BF)
            at = (a * 16 + s * 2) * 8
            out_ref[to, 32:48, :] = part[at : at + 16, :].astype(BF)


def attend(w, got, v2):
    vmem = pl.BlockSpec(memory_space=pltpu.VMEM)
    return pl.pallas_call(
        attend_kernel,
        in_specs=[vmem, vmem, vmem],
        out_specs=vmem,
        out_shape=jax.ShapeDtypeStruct((64, 48, 128), BF),
        scratch_shapes=[pltpu.VMEM((2048, 128), F32), pltpu.VMEM((1024, 128), F32)],
        compiler_params=params(12),
        cost_estimate=pl.CostEstimate(
            flops=2 * 384 * 512 * 1024, bytes_accessed=3 * MIB, transcendentals=0
        ),
        name="attend",
    )(w, got, v2)


def columns_kernel(
    me_ref, att_ref, x0, x1, x2, x3, wo, wqkv, wco, w1, w2, out_ref,
    att, x_in, state, col, sems,
):
    def copy(src, dst, sem):
        return pltpu.make_async_copy(src, dst, sems.at[sem])

    get_x = []
    for k, block in enumerate((x0, x1, x2, x3)):
        for side in range(2):
            y = me_ref[0] if side == 0 else 1 - me_ref[0]
            at = pl.multiple_of((y * 4 + (me_ref[1] ^ k)) * 16, 16)
            get_x.append(copy(block.at[side], x_in.at[:, pl.ds(at, 16), :], 2 + 2 * k + side))
            get_x[-1].start()
    low = low_lanes((8, 8, 128))

    def place(i, tile, first, second):
        top = jnp.where(low, first, pltpu.roll(second, 64, 2))
        bottom = jnp.where(low, pltpu.roll(first, 64, 2), second)
        both = jnp.concatenate([top, bottom], axis=1).reshape(128, 128).astype(BF)
        att[i * 128 : i * 128 + 128, tile * 128 : tile * 128 + 128] = both

    for z in range(4):
        for pair in range(2):
            first = att_ref[:, 0, z, pair * 16 : pair * 16 + 16, :].astype(F32)
            second = att_ref[:, 1, z, pair * 16 : pair * 16 + 16, :].astype(F32)
            for n in range(2):
                rows = slice(n * 8, n * 8 + 8)
                place(pair * 2 + n, FULL[z], first[:, rows], second[:, rows])
    for z in (0, 2):
        for y in range(2):
            first = att_ref[:, y, z, 32:48, :].astype(F32)
            second = att_ref[:, y, z + 1, 32:48, :].astype(F32)
            for n in range(2):
                rows = slice(n * 8, n * 8 + 8)
                place(y * 2 + n, HALF[z], first[:, rows], second[:, rows])
    low = low_lanes((128, 128))
    for block in get_x:
        block.wait()
    after_rows = (x_in[...].reshape(512, D).astype(F32) + dot32(att[...], wo[...])).astype(BF)
    state[...] = after_rows
    normed = normalize(after_rows.astype(F32))
    for t in range(3):
        col[:, t * D : t * D + D] = dot32(normed, wqkv[:, t * D : t * D + D]).astype(BF)
    zero = jnp.zeros((128, 128), BF)
    for i in range(4):
        rows = slice(i * 128, i * 128 + 128)
        for t in range(6):
            q = col[rows, t * 128 : t * 128 + 128]
            k = col[rows, D + t * 128 : D + t * 128 + 128]
            v = col[rows, 2 * D + t * 128 : 2 * D + t * 128 + 128]
            pair = jnp.concatenate([jnp.where(low, q, zero), jnp.where(low, zero, q)], axis=0)
            s = dot_t(pair, k) * (1.0 / math.sqrt(DH))
            e = jnp.exp(s - jnp.max(s, axis=-1, keepdims=True))
            w = (e / jnp.sum(e, axis=-1, keepdims=True)).astype(BF)
            o = dot32(w, v)
            att[rows, t * 128 : t * 128 + 128] = jnp.where(low, o[:128], o[128:]).astype(BF)
    after_cols = (state[...].astype(F32) + dot32(att[...], wco[...])).astype(BF)
    state[...] = after_cols
    normed = normalize(after_cols.astype(F32))
    total = after_cols.astype(F32)
    for t in range(4):
        hidden = jax.nn.gelu(dot32(normed, w1[:, t * D : t * D + D])).astype(BF)
        total += dot32(hidden, w2[t * D : t * D + D, :])
    out = total.astype(BF)
    for i in range(4):
        out_ref[:, i] = out[i * 128 : i * 128 + 128].reshape(8, 16, D)


def columns(me, att, x, wo, wqkv, wco, w1, w2):
    vmem = pl.BlockSpec(memory_space=pltpu.VMEM)
    anywhere = pl.BlockSpec(memory_space=pl.ANY)
    return pl.pallas_call(
        columns_kernel,
        in_specs=[pl.BlockSpec(memory_space=pltpu.SMEM), vmem]
        + [anywhere] * 4
        + [vmem] * 5,
        out_specs=vmem,
        out_shape=jax.ShapeDtypeStruct((8, 4, 16, D), BF),
        scratch_shapes=[
            pltpu.VMEM((512, D), BF),
            pltpu.VMEM((4, 128, D), BF),
            pltpu.VMEM((512, D), BF),
            pltpu.VMEM((512, 3 * D), BF),
            pltpu.SemaphoreType.DMA((11,)),
        ],
        compiler_params=params(24),
        cost_estimate=pl.CostEstimate(
            flops=8 * 10**9, bytes_accessed=18 * MIB, transcendentals=3 * MIB
        ),
        name="columns",
    )(me, att, *x, wo, wqkv, wco, w1, w2)


def per_device(x, row_qkv, row_out, col_qkv, col_out, ff_in, ff_out):
    barrier = lax.optimization_barrier
    swap = [(0, 1), (1, 0)]
    y_me, x_me = lax.axis_index("y_lo"), lax.axis_index("x")
    halves = x.reshape(16, 2, 2, 8, D)
    far = lax.ppermute(lax.dynamic_index_in_dim(halves, 1 - y_me, 2, False), "y_lo", swap)
    me = jnp.stack([y_me, x_me]).astype(jnp.int32)
    proj, x, far, me = barrier((project(x.reshape(512, D), row_qkv), x, far, me))
    got = lax.all_to_all(proj, ("y_hi", "z"), 0, 0, tiled=True)
    mine = lax.dynamic_index_in_dim(x.reshape(16, 2, 2, 8, D), y_me, 2, False)
    x_cols = jnp.stack([mine, far]).reshape(2, 16, 2, 4, 2, D)
    x_cols = x_cols.transpose(3, 0, 2, 4, 1, 5).reshape(4, 2, 4, 16, D)
    near = []
    for k in range(4):
        block = lax.dynamic_index_in_dim(x_cols, x_me ^ k, 0, False)
        near.append(lax.ppermute(block, "x", [(i, i ^ k) for i in range(4)]) if k else block)
    got, near = barrier((got, near))
    k2 = lax.ppermute(got[:, KEY : KEY + 512], "core", swap)
    parts, got = barrier((scores(got, k2), got))
    parts = lax.all_to_all(parts, SEQ, 0, 0, tiled=True)
    v2 = lax.ppermute(got[:, VALUE : VALUE + 512], "core", swap)
    parts, v2 = barrier((parts, v2))
    shares = lax.all_to_all(softmax(parts), SEQ, 0, 0, tiled=True)
    att = lax.all_to_all(attend(shares, got, v2), CHIPS, 0, 0, tiled=True)
    att = att.reshape(8, 2, 4, 48, 128)
    out = columns(me, att, near, row_out, col_qkv, col_out, ff_in, ff_out)
    out = lax.all_to_all(out, SEQ, 0, 0, tiled=True)
    return out.reshape(8, 2, 2, 16, D).transpose(3, 1, 0, 2, 4).reshape(16, 32, D)


def solution(mesh):
    fine = Mesh(mesh.devices.reshape(2, 4, 2, 4, 2), ("y_lo", "x", "y_hi", "z", "core"))
    tokens = P(SEQ, ("y_hi", "z", "core"), None)
    placed = (tokens, P(), P(), P(), P(), P(), P())
    return jax.shard_map(per_device, mesh=fine, in_specs=placed, out_specs=tokens, check_vma=False)
```

```python
import functools
import math

import jax
import jax.numpy as jnp
from jax import lax
from jax.experimental import pallas as pl
from jax.experimental.pallas import tpu as pltpu
from jax.sharding import Mesh, PartitionSpec as P

H = 12
DH = 64
D = H * DH
FF = 4 * D
ROWS = 128
SEQ = ("y_lo", "x")
CHIPS = ("y_lo", "x", "y_hi", "z")
BF = jnp.bfloat16
F32 = jnp.float32
MIB = 1 << 20

FULL = (0, 2, 3, 5)
HALF = (1, 1, 4, 4)

KEY, VALUE, QUERY = 0, 512, 1024


def dot32(a, b):
    return jnp.dot(a, b, preferred_element_type=F32)


def dot_t(a, b):
    return lax.dot_general(a, b, (((1,), (1,)), ((), ())), preferred_element_type=F32)


def dot_tn(a, b):
    return lax.dot_general(a, b, (((0,), (0,)), ((), ())), preferred_element_type=F32)


def swap_halves(v):
    return pltpu.roll(v, 64, 1)


def low_lanes(shape):
    return lax.broadcasted_iota(jnp.int32, shape, len(shape) - 1) % 128 < 64


def normalize(wide):
    centre = jnp.mean(wide, axis=-1, keepdims=True)
    off = wide - centre
    variance = jnp.mean(off * off, axis=-1, keepdims=True)
    return (off * lax.rsqrt(variance + 1e-05)).astype(BF)


def params(mib, **kw):
    return pltpu.CompilerParams(vmem_limit_bytes=mib * MIB, **kw)


def project_kernel(x_hbm, w_hbm, out_hbm, x_ref, w_ref, out_ref, third, sems):
    get_x = pltpu.make_async_copy(x_hbm, x_ref, sems.at[3])
    get_x.start()
    get_w = []
    for t in range(3):
        cols = slice(t * D, t * D + D)
        get_w.append(pltpu.make_async_copy(w_hbm.at[:, cols], w_ref.at[:, cols], sems.at[t]))
    get_w[0].start()
    get_x.wait()
    get_w[1].start()
    get_w[2].start()
    normed = normalize(x_ref[...].astype(F32))
    low = low_lanes((256, 128))
    put = []
    for t in range(3):
        get_w[t].wait()
        val = dot32(normed, w_ref[:, t * D : t * D + D])
        at = (QUERY, KEY, VALUE)[t]
        for tile in range(6):
            first = val[:256, tile * 128 : tile * 128 + 128]
            second = val[256:, tile * 128 : tile * 128 + 128]
            heads = (
                jnp.where(low, first, swap_halves(second)),
                jnp.where(low, swap_halves(first), second),
            )
            if tile in FULL:
                for y in range(2):
                    out_ref[y * 4 + FULL.index(tile), at : at + 256, :] = heads[y].astype(BF)
            else:
                for side in range(2):
                    z = HALF.index(tile) + side
                    if t == 0:
                        third[z * 256 : z * 256 + 256, :] = heads[side]
                    for y in range(2):
                        if t > 0:
                            out_ref[y * 4 + z, at + 256 : at + 512, :] = heads[side].astype(BF)
                        else:
                            picked = [
                                third[pl.ds(z * 256 + y * 2 + n, 64, stride=4), :].reshape(8, 8, 128)
                                for n in range(2)
                            ]
                            part = jnp.concatenate(picked, axis=1).reshape(128, 128).astype(BF)
                            out_ref[y * 4 + z, at + 256 : at + 384, :] = part
        part = pl.ds(at, 384 if t == 0 else 512)
        put.append(
            pltpu.make_async_copy(out_ref.at[:, part], out_hbm.at[:, part], sems.at[4 + t])
        )
        put[t].start()
    for t in range(3):
        put[t].wait()


def project(x, w):
    hbm = pl.BlockSpec(memory_space=pltpu.HBM)
    return pl.pallas_call(
        project_kernel,
        in_specs=[hbm, hbm],
        out_specs=hbm,
        out_shape=jax.ShapeDtypeStruct((8, 1408, 128), BF),
        scratch_shapes=[
            pltpu.VMEM((512, D), BF),
            pltpu.VMEM((D, 3 * D), BF),
            pltpu.VMEM((8, 1408, 128), BF),
            pltpu.VMEM((1024, 128), F32),
            pltpu.SemaphoreType.DMA((7,)),
        ],
        compiler_params=params(58),
        cost_estimate=pl.CostEstimate(
            flops=2 * 512 * D * 3 * D, bytes_accessed=6 * MIB, transcendentals=0
        ),
        name="project",
    )(x, w)


def rows_of(ref, start, size=32):
    return ref[:, start : start + size, :].reshape(8 * size, 128)


def pair_of(refs, start):
    sides = [
        jnp.concatenate([rows_of(ref, at + start + 32 * n) for ref, at in refs], axis=0)
        for n in range(2)
    ]
    return jnp.concatenate(sides, axis=1)


def scores_kernel(got_ref, k2_ref, out_ref):
    for head, size in ((0, 32), (1, 16)):
        total = None
        keys = ((got_ref, KEY + head * 256), (k2_ref, head * 256))
        for r in range(0, 8, 2):
            at = QUERY + head * 256 + r * size
            q = jnp.concatenate(
                [rows_of(got_ref, at, size), rows_of(got_ref, at + size, size)], axis=1
            )
            part = dot_t(q, pair_of(keys, r * 32))
            total = part if total is None else total + part
        at = head * 32
        out_ref[:, at : at + size, :] = total.astype(BF).reshape(8, size, 512)


def scores(got, k2):
    vmem = pl.BlockSpec(memory_space=pltpu.VMEM)
    return pl.pallas_call(
        scores_kernel,
        in_specs=[vmem, vmem],
        out_specs=vmem,
        out_shape=jax.ShapeDtypeStruct((8, 48, 512), BF),
        compiler_params=params(12),
        cost_estimate=pl.CostEstimate(
            flops=2 * 384 * 512 * 1024, bytes_accessed=3 * MIB, transcendentals=0
        ),
        name="scores",
    )(got, k2)


def softmax_kernel(parts_ref, out_ref):
    total = parts_ref[0].astype(F32)
    for s in range(1, 8):
        total += parts_ref[s].astype(F32)
    total *= 1.0 / math.sqrt(DH * ROWS)
    e = jnp.exp(total - jnp.max(total, axis=-1, keepdims=True))
    w = (e * (1.0 / jnp.sum(e, axis=-1, keepdims=True))).astype(BF)
    for s in range(8):
        out_ref[s] = w


def softmax(parts):
    return pl.pallas_call(
        softmax_kernel,
        out_shape=jax.ShapeDtypeStruct((8, 48, 512), BF),
        compiler_params=params(6),
        cost_estimate=pl.CostEstimate(flops=MIB, bytes_accessed=MIB, transcendentals=24576),
        name="softmax",
    )(parts)


def attend_kernel(w_ref, got_ref, v2_ref, out_ref, whole, part):
    for head, size, dest in ((0, 32, whole), (1, 16, part)):
        at = head * 32
        w = w_ref[:, at : at + size, :].reshape(8 * size, 512)
        values = ((got_ref, VALUE + head * 256), (v2_ref, head * 256))
        for r in range(0, 8, 2):
            got = dot32(w, pair_of(values, r * 32))
            dest[pl.ds(r, 8 * size, stride=8), :] = got[:, :128]
            dest[pl.ds(r + 1, 8 * size, stride=8), :] = got[:, 128:]
    for a in range(8):
        for s in range(8):
            to = s * 8 + a
            at = (a * 32 + s * 4) * 8
            out_ref[to, 0:32, :] = whole[at : at + 32, :].astype(BF)
            at = (a * 16 + s) * 8
            pair = jnp.concatenate([part[at : at + 8, :], part[at + 64 : at + 72, :]], axis=0)
            out_ref[to, 32:48, :] = pair.astype(BF)


def attend(w, got, v2):
    vmem = pl.BlockSpec(memory_space=pltpu.VMEM)
    return pl.pallas_call(
        attend_kernel,
        in_specs=[vmem, vmem, vmem],
        out_specs=vmem,
        out_shape=jax.ShapeDtypeStruct((64, 48, 128), BF),
        scratch_shapes=[pltpu.VMEM((2048, 128), F32), pltpu.VMEM((1024, 128), F32)],
        compiler_params=params(12),
        cost_estimate=pl.CostEstimate(
            flops=2 * 384 * 512 * 1024, bytes_accessed=3 * MIB, transcendentals=0
        ),
        name="attend",
    )(w, got, v2)


def columns_kernel(
    me_ref, att_ref, x0, x1, x2, x3, wo, wqkv, wco, w1, w2, out_ref,
    att, x_in, state, col,
):
    low = low_lanes((8, 8, 128))

    def place(i, tile, first, second):
        top = jnp.where(low, first, pltpu.roll(second, 64, 2))
        bottom = jnp.where(low, pltpu.roll(first, 64, 2), second)
        both = jnp.concatenate([top, bottom], axis=1).reshape(128, 128).astype(BF)
        att[i * 128 : i * 128 + 128, tile * 128 : tile * 128 + 128] = both

    for z in range(4):
        for pair in range(2):
            first = att_ref[:, 0, z, pair * 16 : pair * 16 + 16, :].astype(F32)
            second = att_ref[:, 1, z, pair * 16 : pair * 16 + 16, :].astype(F32)
            for n in range(2):
                rows = slice(n * 8, n * 8 + 8)
                place(pair * 2 + n, FULL[z], first[:, rows], second[:, rows])
    for z in (0, 2):
        for y in range(2):
            first = att_ref[:, y, z, 32:48, :].astype(F32)
            second = att_ref[:, y, z + 1, 32:48, :].astype(F32)
            for n in range(2):
                rows = slice(n * 8, n * 8 + 8)
                place(y * 2 + n, HALF[z], first[:, rows], second[:, rows])
    low = low_lanes((128, 128))
    for k, block in enumerate((x0, x1, x2, x3)):
        for side in range(2):
            y = me_ref[0] if side == 0 else 1 - me_ref[0]
            at = pl.multiple_of((y * 4 + (me_ref[1] ^ k)) * 16, 16)
            for i in range(4):
                x_in[i, pl.ds(at, 16), :] = block[side, i]
    after_rows = (x_in[...].reshape(512, D).astype(F32) + dot32(att[...], wo[...])).astype(BF)
    state[...] = after_rows
    normed = normalize(after_rows.astype(F32))
    for t in range(3):
        col[:, t * D : t * D + D] = dot32(normed, wqkv[:, t * D : t * D + D]).astype(BF)
    zero = jnp.zeros((128, 128), BF)
    for i in range(4):
        rows = slice(i * 128, i * 128 + 128)
        for t in range(6):
            q = col[rows, t * 128 : t * 128 + 128]
            k = col[rows, D + t * 128 : D + t * 128 + 128]
            v = col[rows, 2 * D + t * 128 : 2 * D + t * 128 + 128]
            pair = jnp.concatenate([jnp.where(low, q, zero), jnp.where(low, zero, q)], axis=0)
            s = dot_t(k, pair) * (1.0 / math.sqrt(DH))
            e = jnp.exp(s - jnp.max(s, axis=0, keepdims=True))
            w = (e * (1.0 / jnp.sum(e, axis=0, keepdims=True))).astype(BF)
            o = dot_tn(w, v)
            att[rows, t * 128 : t * 128 + 128] = jnp.where(low, o[:128], o[128:]).astype(BF)
    after_cols = (state[...].astype(F32) + dot32(att[...], wco[...])).astype(BF)
    state[...] = after_cols
    normed = normalize(after_cols.astype(F32))
    total = after_cols.astype(F32)
    for t in range(4):
        hidden = jax.nn.gelu(dot32(normed, w1[:, t * D : t * D + D])).astype(BF)
        total += dot32(hidden, w2[t * D : t * D + D, :])
    out = total.astype(BF)
    for i in range(4):
        out_ref[:, i] = out[i * 128 : i * 128 + 128].reshape(8, 16, D)


def columns(me, att, x, wo, wqkv, wco, w1, w2):
    vmem = pl.BlockSpec(memory_space=pltpu.VMEM)
    return pl.pallas_call(
        columns_kernel,
        in_specs=[pl.BlockSpec(memory_space=pltpu.SMEM)] + [vmem] * 10,
        out_specs=vmem,
        out_shape=jax.ShapeDtypeStruct((8, 4, 16, D), BF),
        scratch_shapes=[
            pltpu.VMEM((512, D), BF),
            pltpu.VMEM((4, 128, D), BF),
            pltpu.VMEM((512, D), BF),
            pltpu.VMEM((512, 3 * D), BF),
        ],
        compiler_params=params(24),
        cost_estimate=pl.CostEstimate(
            flops=8 * 10**9, bytes_accessed=18 * MIB, transcendentals=3 * MIB
        ),
        name="columns",
    )(me, att, *x, wo, wqkv, wco, w1, w2)


def per_device(x, row_qkv, row_out, col_qkv, col_out, ff_in, ff_out):
    barrier = lax.optimization_barrier
    swap = [(0, 1), (1, 0)]
    y_me, x_me = lax.axis_index("y_lo"), lax.axis_index("x")
    halves = x.reshape(16, 2, 16, D)
    far = lax.ppermute(lax.dynamic_index_in_dim(halves, 1 - y_me, 1, False), "y_lo", swap)
    me = jnp.stack([y_me, x_me]).astype(jnp.int32)
    proj, x, far, me = barrier((project(x.reshape(512, D), row_qkv), x, far, me))
    got = lax.all_to_all(proj, ("y_hi", "z"), 0, 0, tiled=True)
    mine = lax.dynamic_index_in_dim(x.reshape(16, 2, 16, D), y_me, 1, False)
    x_cols = jnp.stack([mine, far]).reshape(2, 16, 4, 4, D).transpose(2, 0, 3, 1, 4)
    near = []
    for k in range(4):
        block = lax.dynamic_index_in_dim(x_cols, x_me ^ k, 0, False)
        near.append(lax.ppermute(block, "x", [(i, i ^ k) for i in range(4)]) if k else block)
    got, near = barrier((got, near))
    k2 = lax.ppermute(got[:, KEY : KEY + 512], "core", swap)
    parts, got = barrier((scores(got, k2), got))
    parts = lax.all_to_all(parts, SEQ, 0, 0, tiled=True)
    v2 = lax.ppermute(got[:, VALUE : VALUE + 512], "core", swap)
    parts, v2 = barrier((parts, v2))
    shares = lax.all_to_all(softmax(parts), SEQ, 0, 0, tiled=True)
    att = lax.all_to_all(attend(shares, got, v2), CHIPS, 0, 0, tiled=True)
    att = att.reshape(8, 2, 4, 48, 128)
    out = columns(me, att, near, row_out, col_qkv, col_out, ff_in, ff_out)
    out = lax.all_to_all(out, SEQ, 0, 0, tiled=True)
    return out.transpose(2, 0, 1, 3).reshape(16, 32, D)


def solution(mesh):
    fine = Mesh(mesh.devices.reshape(2, 4, 2, 4, 2), ("y_lo", "x", "y_hi", "z", "core"))
    tokens = P(SEQ, ("y_hi", "z", "core"), None)
    placed = (tokens, P(), P(), P(), P(), P(), P())
    return jax.shard_map(per_device, mesh=fine, in_specs=placed, out_specs=tokens, check_vma=False)
```

```python
import functools
import math

import jax
import jax.numpy as jnp
from jax import lax
from jax.experimental import pallas as pl
from jax.experimental.pallas import tpu as pltpu
from jax.sharding import Mesh, PartitionSpec as P

H = 12
DH = 64
D = H * DH
FF = 4 * D
ROWS = 128
SEQ = ("y_lo", "x")
CHIPS = ("y_lo", "x", "y_hi", "z")
BF = jnp.bfloat16
F32 = jnp.float32
MIB = 1 << 20

FULL = (0, 2, 3, 5)
HALF = (1, 1, 4, 4)

KEY, VALUE, QUERY = 0, 512, 1024


def dot32(a, b):
    return jnp.dot(a, b, preferred_element_type=F32)


def dot_t(a, b):
    return lax.dot_general(a, b, (((1,), (1,)), ((), ())), preferred_element_type=F32)


def dot_tn(a, b):
    return lax.dot_general(a, b, (((0,), (0,)), ((), ())), preferred_element_type=F32)


def swap_halves(v):
    return pltpu.roll(v, 64, 1)


def low_lanes(shape):
    return lax.broadcasted_iota(jnp.int32, shape, len(shape) - 1) % 128 < 64


def normalize(wide):
    centre = jnp.mean(wide, axis=-1, keepdims=True)
    off = wide - centre
    variance = jnp.mean(off * off, axis=-1, keepdims=True)
    return (off * lax.rsqrt(variance + 1e-05)).astype(BF)


def params(mib, **kw):
    return pltpu.CompilerParams(vmem_limit_bytes=mib * MIB, **kw)


def project_kernel(x_hbm, w_hbm, out_hbm, x_ref, w_ref, out_ref, third, sems):
    get_x = pltpu.make_async_copy(x_hbm, x_ref, sems.at[3])
    get_x.start()
    get_w = []
    for t in range(3):
        cols = slice(t * D, t * D + D)
        get_w.append(pltpu.make_async_copy(w_hbm.at[:, cols], w_ref.at[:, cols], sems.at[t]))
    get_w[0].start()
    get_x.wait()
    get_w[1].start()
    get_w[2].start()
    normed = normalize(x_ref[...].astype(F32))
    low = low_lanes((256, 128))
    put = []
    for t in range(3):
        get_w[t].wait()
        val = dot32(normed, w_ref[:, t * D : t * D + D])
        at = (QUERY, KEY, VALUE)[t]
        for tile in range(6):
            first = val[:256, tile * 128 : tile * 128 + 128]
            second = val[256:, tile * 128 : tile * 128 + 128]
            heads = (
                jnp.where(low, first, swap_halves(second)),
                jnp.where(low, swap_halves(first), second),
            )
            if tile in FULL:
                for y in range(2):
                    out_ref[y * 4 + FULL.index(tile), at : at + 256, :] = heads[y].astype(BF)
            else:
                for side in range(2):
                    z = HALF.index(tile) + side
                    if t == 0:
                        third[z * 256 : z * 256 + 256, :] = heads[side]
                    for y in range(2):
                        if t > 0:
                            out_ref[y * 4 + z, at + 256 : at + 512, :] = heads[side].astype(BF)
                        else:
                            picked = [
                                third[pl.ds(z * 256 + y * 2 + n, 64, stride=4), :].reshape(8, 8, 128)
                                for n in range(2)
                            ]
                            part = jnp.concatenate(picked, axis=1).reshape(128, 128).astype(BF)
                            out_ref[y * 4 + z, at + 256 : at + 384, :] = part
        part = pl.ds(at, 384 if t == 0 else 512)
        put.append(
            pltpu.make_async_copy(out_ref.at[:, part], out_hbm.at[:, part], sems.at[4 + t])
        )
        put[t].start()
    for t in range(3):
        put[t].wait()


def project(x, w):
    hbm = pl.BlockSpec(memory_space=pltpu.HBM)
    return pl.pallas_call(
        project_kernel,
        in_specs=[hbm, hbm],
        out_specs=hbm,
        out_shape=jax.ShapeDtypeStruct((8, 1408, 128), BF),
        scratch_shapes=[
            pltpu.VMEM((512, D), BF),
            pltpu.VMEM((D, 3 * D), BF),
            pltpu.VMEM((8, 1408, 128), BF),
            pltpu.VMEM((1032, 128), F32),
            pltpu.SemaphoreType.DMA((7,)),
        ],
        compiler_params=params(58),
        cost_estimate=pl.CostEstimate(
            flops=2 * 512 * D * 3 * D, bytes_accessed=6 * MIB, transcendentals=0
        ),
        name="project",
    )(x, w)


def rows_of(ref, start, size=32):
    return ref[:, start : start + size, :].reshape(8 * size, 128)


def pair_of(refs, start):
    sides = [
        jnp.concatenate([rows_of(ref, at + start + 32 * n) for ref, at in refs], axis=0)
        for n in range(2)
    ]
    return jnp.concatenate(sides, axis=1)


def scores_kernel(got_ref, k2_ref, out_ref):
    for head, size in ((0, 32), (1, 16)):
        total = None
        keys = ((got_ref, KEY + head * 256), (k2_ref, head * 256))
        for r in range(0, 8, 2):
            at = QUERY + head * 256 + r * size
            q = jnp.concatenate(
                [rows_of(got_ref, at, size), rows_of(got_ref, at + size, size)], axis=1
            )
            part = dot_t(q, pair_of(keys, r * 32))
            total = part if total is None else total + part
        at = head * 32
        out_ref[:, at : at + size, :] = total.astype(BF).reshape(8, size, 512)


def scores(got, k2):
    vmem = pl.BlockSpec(memory_space=pltpu.VMEM)
    return pl.pallas_call(
        scores_kernel,
        in_specs=[vmem, vmem],
        out_specs=vmem,
        out_shape=jax.ShapeDtypeStruct((8, 48, 512), BF),
        compiler_params=params(12),
        cost_estimate=pl.CostEstimate(
            flops=2 * 384 * 512 * 1024, bytes_accessed=3 * MIB, transcendentals=0
        ),
        name="scores",
    )(got, k2)


def softmax_kernel(parts_ref, out_ref):
    total = parts_ref[0].astype(F32)
    for s in range(1, 8):
        total += parts_ref[s].astype(F32)
    total *= 1.0 / math.sqrt(DH * ROWS)
    e = jnp.exp(total - jnp.max(total, axis=-1, keepdims=True))
    w = (e * (1.0 / jnp.sum(e, axis=-1, keepdims=True))).astype(BF)
    for s in range(8):
        out_ref[s] = w


def softmax(parts):
    return pl.pallas_call(
        softmax_kernel,
        out_shape=jax.ShapeDtypeStruct((8, 48, 512), BF),
        compiler_params=params(6),
        cost_estimate=pl.CostEstimate(flops=MIB, bytes_accessed=MIB, transcendentals=24576),
        name="softmax",
    )(parts)


def attend_kernel(w_ref, got_ref, v2_ref, out_ref, whole, part):
    for head, size, dest in ((0, 32, whole), (1, 16, part)):
        at = head * 32
        w = w_ref[:, at : at + size, :].reshape(8 * size, 512)
        values = ((got_ref, VALUE + head * 256), (v2_ref, head * 256))
        for r in range(0, 8, 2):
            got = dot32(w, pair_of(values, r * 32))
            dest[pl.ds(r, 8 * size, stride=8), :] = got[:, :128]
            dest[pl.ds(r + 1, 8 * size, stride=8), :] = got[:, 128:]
    for a in range(8):
        for s in range(8):
            to = s * 8 + a
            at = (a * 32 + s * 4) * 8
            out_ref[to, 0:32, :] = whole[at : at + 32, :].astype(BF)
            at = (a * 16 + s) * 8
            pair = jnp.concatenate([part[at : at + 8, :], part[at + 64 : at + 72, :]], axis=0)
            out_ref[to, 32:48, :] = pair.astype(BF)


def attend(w, got, v2):
    vmem = pl.BlockSpec(memory_space=pltpu.VMEM)
    return pl.pallas_call(
        attend_kernel,
        in_specs=[vmem, vmem, vmem],
        out_specs=vmem,
        out_shape=jax.ShapeDtypeStruct((64, 48, 128), BF),
        scratch_shapes=[pltpu.VMEM((2056, 128), F32), pltpu.VMEM((1032, 128), F32)],
        compiler_params=params(12),
        cost_estimate=pl.CostEstimate(
            flops=2 * 384 * 512 * 1024, bytes_accessed=3 * MIB, transcendentals=0
        ),
        name="attend",
    )(w, got, v2)


def columns_kernel(
    me_ref, att_ref, x0, x1, x2, x3, wo, wqkv, wco, w1, w2, out_ref,
    att, x_in, state, col,
):
    low = low_lanes((8, 8, 128))

    def place(i, tile, first, second):
        top = jnp.where(low, first, pltpu.roll(second, 64, 2))
        bottom = jnp.where(low, pltpu.roll(first, 64, 2), second)
        both = jnp.concatenate([top, bottom], axis=1).reshape(128, 128).astype(BF)
        att[i * 128 : i * 128 + 128, tile * 128 : tile * 128 + 128] = both

    for z in range(4):
        for pair in range(2):
            first = att_ref[:, 0, z, pair * 16 : pair * 16 + 16, :].astype(F32)
            second = att_ref[:, 1, z, pair * 16 : pair * 16 + 16, :].astype(F32)
            for n in range(2):
                rows = slice(n * 8, n * 8 + 8)
                place(pair * 2 + n, FULL[z], first[:, rows], second[:, rows])
    for z in (0, 2):
        for y in range(2):
            first = att_ref[:, y, z, 32:48, :].astype(F32)
            second = att_ref[:, y, z + 1, 32:48, :].astype(F32)
            for n in range(2):
                rows = slice(n * 8, n * 8 + 8)
                place(y * 2 + n, HALF[z], first[:, rows], second[:, rows])
    low = low_lanes((128, 128))
    for k, block in enumerate((x0, x1, x2, x3)):
        for side in range(2):
            y = me_ref[0] if side == 0 else 1 - me_ref[0]
            at = pl.multiple_of((y * 4 + (me_ref[1] ^ k)) * 16, 16)
            for i in range(4):
                x_in[i, pl.ds(at, 16), :] = block[side, i]
    after_rows = (x_in[...].reshape(512, D).astype(F32) + dot32(att[...], wo[...])).astype(BF)
    state[...] = after_rows
    normed = normalize(after_rows.astype(F32))
    for t in range(3):
        col[:, t * D : t * D + D] = dot32(normed, wqkv[:, t * D : t * D + D]).astype(BF)
    zero = jnp.zeros((128, 128), BF)
    for i in range(4):
        rows = slice(i * 128, i * 128 + 128)
        for t in range(6):
            q = col[rows, t * 128 : t * 128 + 128]
            k = col[rows, D + t * 128 : D + t * 128 + 128]
            v = col[rows, 2 * D + t * 128 : 2 * D + t * 128 + 128]
            pair = jnp.concatenate([jnp.where(low, q, zero), jnp.where(low, zero, q)], axis=0)
            s = dot_t(k, pair) * (1.0 / math.sqrt(DH))
            e = jnp.exp(s - jnp.max(s, axis=0, keepdims=True))
            w = (e * (1.0 / jnp.sum(e, axis=0, keepdims=True))).astype(BF)
            o = dot_tn(w, v)
            att[rows, t * 128 : t * 128 + 128] = jnp.where(low, o[:128], o[128:]).astype(BF)
    after_cols = (state[...].astype(F32) + dot32(att[...], wco[...])).astype(BF)
    state[...] = after_cols
    normed = normalize(after_cols.astype(F32))
    total = after_cols.astype(F32)
    for t in range(4):
        hidden = jax.nn.gelu(dot32(normed, w1[:, t * D : t * D + D])).astype(BF)
        total += dot32(hidden, w2[t * D : t * D + D, :])
    out = total.astype(BF)
    for i in range(4):
        out_ref[:, i] = out[i * 128 : i * 128 + 128].reshape(8, 16, D)


def columns(me, att, x, wo, wqkv, wco, w1, w2):
    vmem = pl.BlockSpec(memory_space=pltpu.VMEM)
    return pl.pallas_call(
        columns_kernel,
        in_specs=[pl.BlockSpec(memory_space=pltpu.SMEM)] + [vmem] * 10,
        out_specs=vmem,
        out_shape=jax.ShapeDtypeStruct((8, 4, 16, D), BF),
        scratch_shapes=[
            pltpu.VMEM((512, D), BF),
            pltpu.VMEM((4, 128, D), BF),
            pltpu.VMEM((512, D), BF),
            pltpu.VMEM((512, 3 * D), BF),
        ],
        compiler_params=params(24),
        cost_estimate=pl.CostEstimate(
            flops=8 * 10**9, bytes_accessed=18 * MIB, transcendentals=3 * MIB
        ),
        name="columns",
    )(me, att, *x, wo, wqkv, wco, w1, w2)


def per_device(x, row_qkv, row_out, col_qkv, col_out, ff_in, ff_out):
    barrier = lax.optimization_barrier
    swap = [(0, 1), (1, 0)]
    y_me, x_me = lax.axis_index("y_lo"), lax.axis_index("x")
    halves = x.reshape(16, 2, 16, D)
    far = lax.ppermute(lax.dynamic_index_in_dim(halves, 1 - y_me, 1, False), "y_lo", swap)
    me = jnp.stack([y_me, x_me]).astype(jnp.int32)
    proj, x, far, me = barrier((project(x.reshape(512, D), row_qkv), x, far, me))
    got = lax.all_to_all(proj, ("y_hi", "z"), 0, 0, tiled=True)
    mine = lax.dynamic_index_in_dim(x.reshape(16, 2, 16, D), y_me, 1, False)
    x_cols = jnp.stack([mine, far]).reshape(2, 16, 4, 4, D).transpose(2, 0, 3, 1, 4)
    near = []
    for k in range(4):
        block = lax.dynamic_index_in_dim(x_cols, x_me ^ k, 0, False)
        near.append(lax.ppermute(block, "x", [(i, i ^ k) for i in range(4)]) if k else block)
    got, near = barrier((got, near))
    k2 = lax.ppermute(got[:, KEY : KEY + 512], "core", swap)
    parts, got = barrier((scores(got, k2), got))
    parts = lax.all_to_all(parts, SEQ, 0, 0, tiled=True)
    v2 = lax.ppermute(got[:, VALUE : VALUE + 512], "core", swap)
    parts, v2 = barrier((parts, v2))
    shares = lax.all_to_all(softmax(parts), SEQ, 0, 0, tiled=True)
    att = lax.all_to_all(attend(shares, got, v2), CHIPS, 0, 0, tiled=True)
    att = att.reshape(8, 2, 4, 48, 128)
    out = columns(me, att, near, row_out, col_qkv, col_out, ff_in, ff_out)
    out = lax.all_to_all(out, SEQ, 0, 0, tiled=True)
    return out.transpose(2, 0, 1, 3).reshape(16, 32, D)


def solution(mesh):
    fine = Mesh(mesh.devices.reshape(2, 4, 2, 4, 2), ("y_lo", "x", "y_hi", "z", "core"))
    tokens = P(SEQ, ("y_hi", "z", "core"), None)
    placed = (tokens, P(), P(), P(), P(), P(), P())
    return jax.shard_map(per_device, mesh=fine, in_specs=placed, out_specs=tokens, check_vma=False)
```

```python
import functools
import math

import jax
import jax.numpy as jnp
from jax import lax
from jax.experimental import pallas as pl
from jax.experimental.pallas import tpu as pltpu
from jax.sharding import Mesh, PartitionSpec as P

H = 12
DH = 64
D = H * DH
FF = 4 * D
ROWS = 128
SEQ = ("y_lo", "x")
CHIPS = ("y_lo", "x", "y_hi", "z")
BF = jnp.bfloat16
F32 = jnp.float32
MIB = 1 << 20

FULL = (0, 2, 3, 5)
HALF = (1, 1, 4, 4)

KEY, VALUE, QUERY = 0, 512, 1024


def dot32(a, b):
    return jnp.dot(a, b, preferred_element_type=F32)


def dot_t(a, b):
    return lax.dot_general(a, b, (((1,), (1,)), ((), ())), preferred_element_type=F32)


def dot_tn(a, b):
    return lax.dot_general(a, b, (((0,), (0,)), ((), ())), preferred_element_type=F32)


def swap_halves(v):
    return pltpu.roll(v, 64, 1)


def low_lanes(shape):
    return lax.broadcasted_iota(jnp.int32, shape, len(shape) - 1) % 128 < 64


def normalize(wide):
    centre = jnp.mean(wide, axis=-1, keepdims=True)
    off = wide - centre
    variance = jnp.mean(off * off, axis=-1, keepdims=True)
    return (off * lax.rsqrt(variance + 1e-05)).astype(BF)


def params(mib, **kw):
    return pltpu.CompilerParams(vmem_limit_bytes=mib * MIB, **kw)


def take_far_kernel(x_hbm, out_ref, sem):
    at = pl.multiple_of((1 - lax.axis_index("y_lo")) * 16, 16)
    copy = pltpu.make_async_copy(x_hbm.at[:, pl.ds(at, 16), :], out_ref, sem)
    copy.start()
    copy.wait()


def take_far(x):
    anywhere = pl.BlockSpec(memory_space=pl.ANY)
    return pl.pallas_call(
        take_far_kernel,
        in_specs=[anywhere],
        out_specs=pl.BlockSpec(memory_space=pltpu.VMEM),
        out_shape=jax.ShapeDtypeStruct((16, 16, D), BF),
        scratch_shapes=[pltpu.SemaphoreType.DMA],
        compiler_params=params(8),
        cost_estimate=pl.CostEstimate(flops=0, bytes_accessed=MIB, transcendentals=0),
        name="take_far",
    )(x)


def project_kernel(x_hbm, w_hbm, out_hbm, x_ref, w_ref, out_ref, third, sems):
    get_x = pltpu.make_async_copy(x_hbm, x_ref, sems.at[3])
    get_x.start()
    get_w = []
    for t in range(3):
        cols = slice(t * D, t * D + D)
        get_w.append(pltpu.make_async_copy(w_hbm.at[:, cols], w_ref.at[:, cols], sems.at[t]))
    get_w[0].start()
    get_x.wait()
    get_w[1].start()
    get_w[2].start()
    normed = normalize(x_ref[...].astype(F32))
    low = low_lanes((256, 128))
    put = []
    for t in range(3):
        get_w[t].wait()
        val = dot32(normed, w_ref[:, t * D : t * D + D])
        at = (QUERY, KEY, VALUE)[t]
        for tile in range(6):
            first = val[:256, tile * 128 : tile * 128 + 128]
            second = val[256:, tile * 128 : tile * 128 + 128]
            heads = (
                jnp.where(low, first, swap_halves(second)),
                jnp.where(low, swap_halves(first), second),
            )
            if tile in FULL:
                for y in range(2):
                    out_ref[y * 4 + FULL.index(tile), at : at + 256, :] = heads[y].astype(BF)
            else:
                for side in range(2):
                    z = HALF.index(tile) + side
                    if t == 0:
                        third[z * 256 : z * 256 + 256, :] = heads[side]
                    for y in range(2):
                        if t > 0:
                            out_ref[y * 4 + z, at + 256 : at + 512, :] = heads[side].astype(BF)
                        else:
                            picked = [
                                third[pl.ds(z * 256 + y * 2 + n, 64, stride=4), :].reshape(8, 8, 128)
                                for n in range(2)
                            ]
                            part = jnp.concatenate(picked, axis=1).reshape(128, 128).astype(BF)
                            out_ref[y * 4 + z, at + 256 : at + 384, :] = part
        part = pl.ds(at, 384 if t == 0 else 512)
        put.append(
            pltpu.make_async_copy(out_ref.at[:, part], out_hbm.at[:, part], sems.at[4 + t])
        )
        put[t].start()
    for t in range(3):
        put[t].wait()


def project(x, w):
    hbm = pl.BlockSpec(memory_space=pltpu.HBM)
    return pl.pallas_call(
        project_kernel,
        in_specs=[hbm, hbm],
        out_specs=hbm,
        out_shape=jax.ShapeDtypeStruct((8, 1408, 128), BF),
        scratch_shapes=[
            pltpu.VMEM((512, D), BF),
            pltpu.VMEM((D, 3 * D), BF),
            pltpu.VMEM((8, 1408, 128), BF),
            pltpu.VMEM((1032, 128), F32),
            pltpu.SemaphoreType.DMA((7,)),
        ],
        compiler_params=params(58),
        cost_estimate=pl.CostEstimate(
            flops=2 * 512 * D * 3 * D, bytes_accessed=6 * MIB, transcendentals=0
        ),
        name="project",
    )(x, w)


def rows_of(ref, start, size=32):
    return ref[:, start : start + size, :].reshape(8 * size, 128)


def pair_of(refs, start):
    sides = [
        jnp.concatenate([rows_of(ref, at + start + 32 * n) for ref, at in refs], axis=0)
        for n in range(2)
    ]
    return jnp.concatenate(sides, axis=1)


def scores_kernel(got_ref, k2_ref, out_ref):
    for head, size in ((0, 32), (1, 16)):
        total = None
        keys = ((got_ref, KEY + head * 256), (k2_ref, head * 256))
        for r in range(0, 8, 2):
            at = QUERY + head * 256 + r * size
            q = jnp.concatenate(
                [rows_of(got_ref, at, size), rows_of(got_ref, at + size, size)], axis=1
            )
            part = dot_t(q, pair_of(keys, r * 32))
            total = part if total is None else total + part
        at = head * 32
        out_ref[:, at : at + size, :] = total.astype(BF).reshape(8, size, 512)


def scores(got, k2):
    vmem = pl.BlockSpec(memory_space=pltpu.VMEM)
    return pl.pallas_call(
        scores_kernel,
        in_specs=[vmem, vmem],
        out_specs=vmem,
        out_shape=jax.ShapeDtypeStruct((8, 48, 512), BF),
        compiler_params=params(12),
        cost_estimate=pl.CostEstimate(
            flops=2 * 384 * 512 * 1024, bytes_accessed=3 * MIB, transcendentals=0
        ),
        name="scores",
    )(got, k2)


def softmax_kernel(parts_ref, out_ref):
    total = parts_ref[0].astype(F32)
    for s in range(1, 8):
        total += parts_ref[s].astype(F32)
    total *= 1.0 / math.sqrt(DH * ROWS)
    e = jnp.exp(total - jnp.max(total, axis=-1, keepdims=True))
    w = (e * (1.0 / jnp.sum(e, axis=-1, keepdims=True))).astype(BF)
    for s in range(8):
        out_ref[s] = w


def softmax(parts):
    return pl.pallas_call(
        softmax_kernel,
        out_shape=jax.ShapeDtypeStruct((8, 48, 512), BF),
        compiler_params=params(6),
        cost_estimate=pl.CostEstimate(flops=MIB, bytes_accessed=MIB, transcendentals=24576),
        name="softmax",
    )(parts)


def attend_kernel(w_ref, got_ref, v2_ref, out_ref, whole, part):
    for head, size, dest in ((0, 32, whole), (1, 16, part)):
        at = head * 32
        w = w_ref[:, at : at + size, :].reshape(8 * size, 512)
        values = ((got_ref, VALUE + head * 256), (v2_ref, head * 256))
        for r in range(0, 8, 2):
            got = dot32(w, pair_of(values, r * 32))
            dest[pl.ds(r, 8 * size, stride=8), :] = got[:, :128]
            dest[pl.ds(r + 1, 8 * size, stride=8), :] = got[:, 128:]
    for a in range(8):
        for s in range(8):
            to = s * 8 + a
            at = (a * 32 + s * 4) * 8
            out_ref[to, 0:32, :] = whole[at : at + 32, :].astype(BF)
            at = (a * 16 + s) * 8
            pair = jnp.concatenate([part[at : at + 8, :], part[at + 64 : at + 72, :]], axis=0)
            out_ref[to, 32:48, :] = pair.astype(BF)


def attend(w, got, v2):
    vmem = pl.BlockSpec(memory_space=pltpu.VMEM)
    return pl.pallas_call(
        attend_kernel,
        in_specs=[vmem, vmem, vmem],
        out_specs=vmem,
        out_shape=jax.ShapeDtypeStruct((64, 48, 128), BF),
        scratch_shapes=[pltpu.VMEM((2056, 128), F32), pltpu.VMEM((1032, 128), F32)],
        compiler_params=params(12),
        cost_estimate=pl.CostEstimate(
            flops=2 * 384 * 512 * 1024, bytes_accessed=3 * MIB, transcendentals=0
        ),
        name="attend",
    )(w, got, v2)


def columns_kernel(
    me_ref, att_ref, x0, x1, x2, x3, wo, wqkv, wco, w1, w2, out_ref,
    att, x_in, state, col,
):
    low = low_lanes((8, 8, 128))

    def place(i, tile, first, second):
        top = jnp.where(low, first, pltpu.roll(second, 64, 2))
        bottom = jnp.where(low, pltpu.roll(first, 64, 2), second)
        both = jnp.concatenate([top, bottom], axis=1).reshape(128, 128).astype(BF)
        att[i * 128 : i * 128 + 128, tile * 128 : tile * 128 + 128] = both

    for z in range(4):
        for pair in range(2):
            first = att_ref[:, 0, z, pair * 16 : pair * 16 + 16, :].astype(F32)
            second = att_ref[:, 1, z, pair * 16 : pair * 16 + 16, :].astype(F32)
            for n in range(2):
                rows = slice(n * 8, n * 8 + 8)
                place(pair * 2 + n, FULL[z], first[:, rows], second[:, rows])
    for z in (0, 2):
        for y in range(2):
            first = att_ref[:, y, z, 32:48, :].astype(F32)
            second = att_ref[:, y, z + 1, 32:48, :].astype(F32)
            for n in range(2):
                rows = slice(n * 8, n * 8 + 8)
                place(y * 2 + n, HALF[z], first[:, rows], second[:, rows])
    low = low_lanes((128, 128))
    for k, block in enumerate((x0, x1, x2, x3)):
        for side in range(2):
            y = me_ref[0] if side == 0 else 1 - me_ref[0]
            at = pl.multiple_of((y * 4 + (me_ref[1] ^ k)) * 16, 16)
            for i in range(4):
                x_in[i, pl.ds(at, 16), :] = block[side, i]
    after_rows = (x_in[...].reshape(512, D).astype(F32) + dot32(att[...], wo[...])).astype(BF)
    state[...] = after_rows
    normed = normalize(after_rows.astype(F32))
    for t in range(3):
        col[:, t * D : t * D + D] = dot32(normed, wqkv[:, t * D : t * D + D]).astype(BF)
    zero = jnp.zeros((128, 128), BF)
    for i in range(4):
        rows = slice(i * 128, i * 128 + 128)
        for t in range(6):
            q = col[rows, t * 128 : t * 128 + 128]
            k = col[rows, D + t * 128 : D + t * 128 + 128]
            v = col[rows, 2 * D + t * 128 : 2 * D + t * 128 + 128]
            pair = jnp.concatenate([jnp.where(low, q, zero), jnp.where(low, zero, q)], axis=0)
            s = dot_t(k, pair) * (1.0 / math.sqrt(DH))
            e = jnp.exp(s - jnp.max(s, axis=0, keepdims=True))
            w = (e * (1.0 / jnp.sum(e, axis=0, keepdims=True))).astype(BF)
            o = dot_tn(w, v)
            att[rows, t * 128 : t * 128 + 128] = jnp.where(low, o[:128], o[128:]).astype(BF)
    after_cols = (state[...].astype(F32) + dot32(att[...], wco[...])).astype(BF)
    state[...] = after_cols
    normed = normalize(after_cols.astype(F32))
    total = after_cols.astype(F32)
    for t in range(4):
        hidden = jax.nn.gelu(dot32(normed, w1[:, t * D : t * D + D])).astype(BF)
        total += dot32(hidden, w2[t * D : t * D + D, :])
    out = total.astype(BF)
    for i in range(4):
        out_ref[:, i] = out[i * 128 : i * 128 + 128].reshape(8, 16, D)


def columns(me, att, x, wo, wqkv, wco, w1, w2):
    vmem = pl.BlockSpec(memory_space=pltpu.VMEM)
    return pl.pallas_call(
        columns_kernel,
        in_specs=[pl.BlockSpec(memory_space=pltpu.SMEM)] + [vmem] * 10,
        out_specs=vmem,
        out_shape=jax.ShapeDtypeStruct((8, 4, 16, D), BF),
        scratch_shapes=[
            pltpu.VMEM((512, D), BF),
            pltpu.VMEM((4, 128, D), BF),
            pltpu.VMEM((512, D), BF),
            pltpu.VMEM((512, 3 * D), BF),
        ],
        compiler_params=params(24),
        cost_estimate=pl.CostEstimate(
            flops=8 * 10**9, bytes_accessed=18 * MIB, transcendentals=3 * MIB
        ),
        name="columns",
    )(me, att, *x, wo, wqkv, wco, w1, w2)


def per_device(x, row_qkv, row_out, col_qkv, col_out, ff_in, ff_out):
    barrier = lax.optimization_barrier
    swap = [(0, 1), (1, 0)]
    y_me, x_me = lax.axis_index("y_lo"), lax.axis_index("x")
    far = lax.ppermute(take_far(x), "y_lo", swap)
    me = jnp.stack([y_me, x_me]).astype(jnp.int32)
    proj, x, far, me = barrier((project(x.reshape(512, D), row_qkv), x, far, me))
    got = lax.all_to_all(proj, ("y_hi", "z"), 0, 0, tiled=True)
    mine = lax.dynamic_index_in_dim(x.reshape(16, 2, 16, D), y_me, 1, False)
    x_cols = jnp.stack([mine, far]).reshape(2, 16, 4, 4, D).transpose(2, 0, 3, 1, 4)
    near = []
    for k in range(4):
        block = lax.dynamic_index_in_dim(x_cols, x_me ^ k, 0, False)
        near.append(lax.ppermute(block, "x", [(i, i ^ k) for i in range(4)]) if k else block)
    got, near = barrier((got, near))
    k2 = lax.ppermute(got[:, KEY : KEY + 512], "core", swap)
    parts, got = barrier((scores(got, k2), got))
    parts = lax.all_to_all(parts, SEQ, 0, 0, tiled=True)
    v2 = lax.ppermute(got[:, VALUE : VALUE + 512], "core", swap)
    parts, v2 = barrier((parts, v2))
    shares = lax.all_to_all(softmax(parts), SEQ, 0, 0, tiled=True)
    att = lax.all_to_all(attend(shares, got, v2), CHIPS, 0, 0, tiled=True)
    att = att.reshape(8, 2, 4, 48, 128)
    out = columns(me, att, near, row_out, col_qkv, col_out, ff_in, ff_out)
    out = lax.all_to_all(out, SEQ, 0, 0, tiled=True)
    return out.transpose(2, 0, 1, 3).reshape(16, 32, D)


def solution(mesh):
    fine = Mesh(mesh.devices.reshape(2, 4, 2, 4, 2), ("y_lo", "x", "y_hi", "z", "core"))
    tokens = P(SEQ, ("y_hi", "z", "core"), None)
    placed = (tokens, P(), P(), P(), P(), P(), P())
    return jax.shard_map(per_device, mesh=fine, in_specs=placed, out_specs=tokens, check_vma=False)
```
